32 devices in a mesh: groups: 2 (over x), ep: 16 (over z, y, core).
Axes of the slice: x: 2, y: 2, z: 4, core: 2. Of those that a mesh axis runs over, the one named last changes fastest.
Arguments:
- thinker_rows: bfloat16 [512, 2048], P(('groups', 'ep')), parts along dimension 0, may hold values from -6 to 6
- expert_ids: int32 [512, 8], P(('groups', 'ep')), parts along dimension 0, may hold values from 0 to 15, all different within a row; in each aligned block of 16 rows (0 to 15, 16 to 31, ...) at most 16 rows name the same one
- gate_weights: float32 [512, 8], P(('groups', 'ep')), parts along dimension 0, may hold values from 0.2 to 1
- w_gate: bfloat16 [16, 2048, 512], P('ep'), may hold values from -0.125 to 0.125
- w_up: bfloat16 [16, 2048, 512], P('ep'), may hold values from -0.125 to 0.125
- w_down: bfloat16 [16, 512, 2048], P('ep'), may hold values from -0.25 to 0.25
- talker_proj: bfloat16 [2048, 1024], replicated, may hold values from -0.125 to 0.125
- talker_slot: int32 [32, 16], P(('groups', 'ep')), parts along dimension 0, may hold values from 0 to 15, each once within a row
- speech_count: int32 [512], P(('groups', 'ep')), parts along dimension 0, may hold values from 0 to 4
- left_context: bfloat16 [512, 6, 1024], P(('groups', 'ep')), parts along dimension 0, may hold values from -6 to 6
- frame_offset: float32 [4, 1024], replicated, may hold values from -6 to 6
- conv_weight: float32 [7, 1024], replicated, may hold values from -2.4 to 2.4
Outputs:
- voice_frames: bfloat16 [512, 4, 1024], P(('groups', 'ep')), parts along dimension 0
The draws below stay inside these ranges and needn't reach their ends.
There are 2 independent parts, one for each index of `groups`. The reference program is written for one: setup_inputs(seed, part) draws one part's arguments, and reference() takes and returns one part's arrays. A program takes and returns all parts, laid end to end along the dimension named above; an argument that names none is the same for every part. Nothing has to cross between parts.
Inputs may be any that keep to these rules, and one draw needn't show every extreme that they name: `expert_ids`: each row names 8 different experts; among the rows of one device no expert is named by more than 16 rows, and in every draw some expert is named by exactly 16 rows of some device. `talker_slot`: each device's row is a permutation of 0 to 15.
All inputs are finite; a program needn't handle non-finite values.
Results may differ from the reference program's by a relative error of at most 0.007.
Values may be sent and summed in bfloat16 or wider, within the bound.
A program may use at most 64 MiB of HBM per device.

```python
import math
import jax
import jax.numpy as jnp
import numpy as np
from jax import lax

D = 2048
MOE_FF = 512
TD = 1024
TOPK = 8
KW = 7
FR = 4
HCAP = 1
EXPERTS = 16
OWNERS = 16
STR_DEV = 16
STREAMS = 256
CAP = 16


def place_ends(drawn, own_key, smallest, top_value):
    shape = drawn.shape
    spot = [jax.random.randint(jax.random.fold_in(own_key, axis), (), 0, shape[axis]) for axis in range(len(shape))]
    drawn = drawn.at[tuple(spot)].set(smallest)
    longest = shape.index(max(shape))
    spot[longest] = (spot[longest] + 1) % shape[longest]
    return drawn.at[tuple(spot)].set(top_value)


def levels(own_key, extent, cuts, low, largest):
    factor_of = 1.0
    for dim, parts in cuts:
        draws = jax.random.uniform(jax.random.fold_in(jax.random.fold_in(own_key, 6), dim), (parts,), jnp.float32, low / len(cuts), largest / len(cuts))
        factor_of = factor_of * jnp.repeat(jnp.exp(draws), extent[dim] // parts).reshape((-1,) + (1,) * (len(extent) - 1 - dim))
    return factor_of


def shared_out(stream_key, own, number, rows, number_of, top, limit, slope):
    order = jax.random.permutation(stream_key, number_of)
    crowded, common = shares(number_of, rows * top, limit, slope, True), shares(number_of, rows * top, limit, slope, False)
    places = jnp.arange(number_of)

    def named(sizes, offset_by):
        used = int((sizes > 0).sum())
        fixed = max(1, used // 4)
        moved = fixed + (places - fixed + offset_by * (used - fixed)) % max(1, number_of - fixed)
        return jnp.zeros((number_of,), jnp.int32).at[order[jnp.where(places < fixed, places, moved)]].set(jnp.asarray(sizes, jnp.int32))

    sizes = jnp.where(number % 4 == 0, named(crowded, number // 4), named(common, number - number // 4 - 1))
    mixed = jax.random.permutation(jax.random.fold_in(own, 3), number_of)
    source_of, receiver = mixed[0:number_of // 2 * 2:2], mixed[1:number_of // 2 * 2:2]
    room = jnp.minimum(sizes[source_of] - 1, limit - sizes[receiver]) // 2
    room = jnp.where((source_of == order[0]) | (receiver == order[0]) | (sizes[receiver] == 0), 0, jnp.maximum(room, 0))
    moved = jax.random.randint(jax.random.fold_in(own, 4), (number_of // 2,), 0, 1 << 20) % (room + 1)
    sizes = sizes.at[source_of].add(-moved).at[receiver].add(moved)
    items = jnp.searchsorted(jnp.cumsum(sizes), jnp.arange(rows * top), side="right").astype(jnp.int32)
    grid = items.reshape(top, rows).T
    grid = grid[jax.random.permutation(jax.random.fold_in(own, 1), rows)]
    offset_by = jax.random.randint(jax.random.fold_in(own, 2), (rows, 1), 0, top)
    return jnp.take_along_axis(grid, (jnp.arange(top)[None, :] + offset_by) % top, axis=1)


def shares(amount, total, bound, skew, full):
    loads = [(1 << 20) // math.isqrt(grade ** skew) + 1 for grade in range(1, amount + 1)]
    largest = bound if full else min(bound, max(-(-total // amount), total * loads[0] // sum(loads)))
    least = 1 if total - largest >= amount - 1 else 0
    holding, surplus = [largest] + [least] * (amount - 1), total - largest - least * (amount - 1)
    while surplus > 0:
        candidates = [i for i in range(1, amount) if holding[i] < largest] or [i for i in range(1, amount) if holding[i] < bound]
        pool, budget = sum([loads[i] for i in candidates]), surplus
        for i in candidates:
            extra = min(bound - holding[i], max(1, budget * loads[i] // pool), surplus)
            holding[i] = holding[i] + extra
            surplus = surplus - extra
    return np.array(holding)


def gaussian(key, shape, scale, reach, shards=(), kind=jnp.bfloat16):
    drawn = jax.random.normal(key, shape, jnp.float32) * scale
    if len(shards) > 0:
        drawn = levels(key, shape, shards, -0.22, 0.18) * drawn
    return jnp.clip(drawn, min=-reach, max=reach).astype(kind)


def setup_inputs(seed: int = 0, part: int = 0) -> dict:
    arg_keys = jax.random.split(jax.random.key(seed), 13)
    part_keys = jax.random.split(jax.random.fold_in(arg_keys[12], part), 13)
    thinker_rows = gaussian(part_keys[0], (STREAMS, D), 1.0, 6.0, ((0, 16),))
    expert_ids_keys = jax.random.split(jax.random.fold_in(part_keys[1], 1), STREAMS // STR_DEV)
    expert_ids_turns = jax.random.permutation(jax.random.fold_in(part_keys[1], 3), STREAMS // STR_DEV)
    expert_ids = jax.vmap(lambda own, number: shared_out(jax.random.fold_in(part_keys[1], 2), own, number, STR_DEV, EXPERTS, TOPK, CAP, 2))(expert_ids_keys, expert_ids_turns).reshape((STREAMS, TOPK))
    gate_weights = jnp.clip(jnp.exp(math.log(1.0) - 1.609438 * jax.random.uniform(part_keys[2], (STREAMS, TOPK), jnp.float32) ** levels(part_keys[2], (STREAMS, TOPK), ((0, 16),), -0.2, 0.2)), 0.2, 1.0)
    w_gate = gaussian(arg_keys[3], (EXPERTS, D, MOE_FF), D ** -0.5, 0.125, ((0, 16),))
    w_up = gaussian(arg_keys[4], (EXPERTS, D, MOE_FF), D ** -0.5, 0.125, ((0, 16),))
    w_down = gaussian(arg_keys[5], (EXPERTS, MOE_FF, D), MOE_FF ** -0.5, 0.25, ((0, 16),))
    talker_proj = gaussian(arg_keys[6], (D, TD), D ** -0.5, 0.125)
    talker_slot = jax.vmap(lambda own: jax.random.permutation(own, STR_DEV))(jax.random.split(part_keys[7], OWNERS)).reshape((OWNERS, STR_DEV)).astype(jnp.int32)
    speech_count = place_ends(jax.random.randint(part_keys[8], (STREAMS,), 0, FR + 1), jax.random.fold_in(part_keys[8], 1), 0, FR).astype(jnp.int32)
    left_context = gaussian(part_keys[9], (STREAMS, KW - 1, TD), 1.0, 6.0, ((0, 16),))
    frame_offset = gaussian(arg_keys[10], (FR, TD), 1.0, 6.0, (), jnp.float32)
    conv_weight = gaussian(arg_keys[11], (KW, TD), 0.4, 2.4, (), jnp.float32)
    return {"thinker_rows": thinker_rows, "expert_ids": expert_ids, "gate_weights": gate_weights, "w_gate": w_gate, "w_up": w_up, "w_down": w_down, "talker_proj": talker_proj, "talker_slot": talker_slot, "speech_count": speech_count, "left_context": left_context, "frame_offset": frame_offset, "conv_weight": conv_weight}


def expert_block(block_rows, gate_mat, up_mat, down_mat):
    gate_act = jnp.dot(block_rows, gate_mat, preferred_element_type=jnp.float32)
    up_act = jnp.dot(block_rows, up_mat, preferred_element_type=jnp.float32)
    inner = (jax.nn.silu(gate_act) * up_act).astype(jnp.bfloat16)
    return jnp.dot(inner, down_mat, preferred_element_type=jnp.float32).astype(jnp.bfloat16)

def project(hidden, talker_proj):
    values = hidden.astype(jnp.float32)
    scaled = values * lax.rsqrt(lax.optimization_barrier(jnp.mean(values * values, axis=-1, keepdims=True)) + 1e-06)
    return jnp.dot(scaled.astype(jnp.bfloat16), talker_proj, preferred_element_type=jnp.float32).astype(jnp.bfloat16)

def vocode(owned, speech_count, left_context, frame_offset, conv_weight):
    frames = owned.astype(jnp.float32)[:, None, :] + frame_offset[None, :, :]
    sequence = jnp.concatenate([left_context.astype(jnp.float32), frames], axis=1)
    taps = conv_weight.shape[0]
    horizon = frame_offset.shape[0]
    result = jnp.zeros_like(frames)
    for offset in range(taps):
        result = result + conv_weight[offset][None, None, :] * sequence[:, offset:offset + horizon, :]
    active = jnp.arange(horizon, dtype=jnp.int32)[None, :, None] < speech_count[:, None, None]
    return jnp.where(active, result, 0.0).astype(jnp.bfloat16)

def reference(thinker_rows, expert_ids, gate_weights, w_gate, w_up, w_down, talker_proj, talker_slot, speech_count, left_context, frame_offset, conv_weight):
    owners = STREAMS // STR_DEV
    blocks = expert_ids.reshape(owners, STR_DEV * TOPK)
    labels = jnp.arange(EXPERTS, dtype=jnp.int32)
    onehot = (blocks[:, :, None] == labels[None, None, :]).astype(jnp.int32)
    position = lax.optimization_barrier(jnp.sum((jnp.cumsum(onehot, axis=1) - onehot) * onehot, axis=2)).reshape(-1).astype(jnp.int32)
    flat_expert = expert_ids.reshape(-1).astype(jnp.int32)
    assigned = jnp.arange(STREAMS * TOPK, dtype=jnp.int32)
    source = assigned // (STR_DEV * TOPK)
    row_index = assigned // TOPK
    padded_rows = jnp.concatenate([thinker_rows, jnp.zeros((1, D), thinker_rows.dtype)], axis=0)

    def run_expert(expert):
        target = jnp.where(flat_expert == expert, source, owners)
        table = jnp.full((owners, CAP), STREAMS, jnp.int32).at[target, position].set(row_index, mode='drop')
        block_rows = padded_rows[table.reshape(-1)]
        return expert_block(block_rows, w_gate[expert], w_up[expert], w_down[expert])
    outputs = lax.map(run_expert, labels).reshape(EXPERTS * owners * CAP, D)
    lookup = (flat_expert * (owners * CAP) + source * CAP + position).reshape(STREAMS, TOPK)
    mixture = thinker_rows.astype(jnp.float32)
    for rank_index in range(TOPK):
        mixture = mixture + gate_weights[:, rank_index, None] * outputs[lookup[:, rank_index]].astype(jnp.float32)
    hidden = mixture.astype(jnp.bfloat16)
    talker_rows = project(hidden, talker_proj)
    slots = talker_slot.reshape(-1).astype(jnp.int32)
    stream_ids = jnp.arange(STREAMS, dtype=jnp.int32)
    owner_index = slots // HCAP * STR_DEV + stream_ids // STR_DEV * HCAP + slots % HCAP
    owned = jnp.zeros((STREAMS, TD), talker_rows.dtype).at[owner_index].set(talker_rows)
    return vocode(owned, speech_count, left_context, frame_offset, conv_weight)
```

```python
import functools

import jax
import jax.numpy as jnp
from jax import lax
from jax.experimental import pallas as pl
from jax.experimental.pallas import tpu as pltpu
from jax.sharding import PartitionSpec as P

CAP = 16
LANES = 128


def expert_block(block_rows, gate_mat, up_mat, down_mat):
    gate_act = jnp.dot(block_rows, gate_mat, preferred_element_type=jnp.float32)
    up_act = jnp.dot(block_rows, up_mat, preferred_element_type=jnp.float32)
    inner = (jax.nn.silu(gate_act) * up_act).astype(jnp.bfloat16)
    return jnp.dot(inner, down_mat, preferred_element_type=jnp.float32).astype(jnp.bfloat16)


def project(hidden, talker_proj):
    values = hidden.astype(jnp.float32)
    scaled = values * lax.rsqrt(jnp.mean(values * values, axis=-1, keepdims=True) + 1e-06)
    return jnp.dot(
        scaled.astype(jnp.bfloat16), talker_proj, preferred_element_type=jnp.float32
    ).astype(jnp.bfloat16)


def vocode(owned, speech_count, left_context, frame_offset, conv_weight):
    frames = owned.astype(jnp.float32)[:, None, :] + frame_offset[None, :, :]
    sequence = jnp.concatenate([left_context.astype(jnp.float32), frames], axis=1)
    taps = conv_weight.shape[0]
    horizon = frame_offset.shape[0]
    result = jnp.zeros_like(frames)
    for offset in range(taps):
        result = (
            result + conv_weight[offset][None, None, :] * sequence[:, offset : offset + horizon, :]
        )
    active = jnp.arange(horizon, dtype=jnp.int32)[None, :, None] < speech_count[:, None, None]
    return jnp.where(active, result, 0.0).astype(jnp.bfloat16)


def slot_positions(expert_ids, experts):
    flat_expert = expert_ids.reshape(-1)
    onehot = (flat_expert[:, None] == jnp.arange(experts, dtype=jnp.int32)[None, :]).astype(
        jnp.int32
    )
    position = jnp.sum((jnp.cumsum(onehot, axis=0) - onehot) * onehot, axis=1)
    return (flat_expert, position)


def run_and_return(buffer, w_gate, w_up, w_down):
    sources, slot_count, features = buffer.shape
    flattened = buffer.reshape(sources * slot_count, features)
    outputs = expert_block(flattened, w_gate[0], w_up[0], w_down[0]).reshape(
        sources, slot_count, features
    )
    return lax.all_to_all(outputs, "ep", split_axis=0, concat_axis=0, tiled=True)


def capacity_path(
    thinker_rows, expert_ids, gate_weights, w_gate, w_up, w_down, talker_proj, talker_slot
):
    devices = lax.axis_size("ep")
    streams_here, features = thinker_rows.shape
    chosen = expert_ids.shape[1]
    flat_expert, position = slot_positions(expert_ids, devices)
    row_index = jnp.arange(streams_here * chosen, dtype=jnp.int32) // chosen
    outgoing = (
        jnp.zeros((devices, CAP, features), jnp.bfloat16)
        .at[flat_expert, position]
        .set(thinker_rows[row_index])
    )
    returned = run_and_return(
        lax.all_to_all(outgoing, "ep", split_axis=0, concat_axis=0, tiled=True),
        w_gate,
        w_up,
        w_down,
    )
    lookup = (
        returned[flat_expert, position].astype(jnp.float32).reshape(streams_here, chosen, features)
    )
    mixture = jnp.sum(gate_weights[:, :, None] * lookup, axis=1)
    hidden = (thinker_rows.astype(jnp.float32) + mixture).astype(jnp.bfloat16)
    slots = talker_slot[0]
    per_owner = streams_here // devices
    talker_rows = project(hidden, talker_proj)
    placed = (
        jnp.zeros_like(talker_rows)
        .at[slots]
        .set(talker_rows)
        .reshape(devices, per_owner, talker_rows.shape[1])
    )
    return lax.all_to_all(placed, "ep", split_axis=0, concat_axis=0, tiled=True).reshape(
        streams_here, talker_rows.shape[1]
    )


def dense_kernel(
    n,
    rows_ref,
    ids_ref,
    gates_ref,
    slot_ref,
    wg_hbm,
    wu_hbm,
    wd_hbm,
    proj_hbm,
    owned_ref,
    wg,
    wu,
    wd,
    proj,
    x_all,
    inner,
    part,
    sib_in,
    pair_out,
    y_in,
    y_out,
    z_in,
    row_out,
    row_in,
    load_sem,
    gz_send,
    gz_recv,
    gy_send,
    gy_recv,
    gs_send,
    gs_recv,
    rs_send,
    rs_recv,
    ry_send,
    ry_recv,
    rz_send,
    rz_recv,
    t_send,
    t_recv,
):
    f32, bf16 = jnp.float32, jnp.bfloat16
    rows, feat = rows_ref.shape
    hid = wg.shape[1]
    width = proj.shape[1]
    line = n // 4
    half = line * rows
    tile = min(256, hid)
    me = lax.axis_index("ep")
    z = me // 4
    within = me % 4
    y = within // 2
    core = within % 2
    y_peer = me + 2 - 4 * y
    sibling = me + 1 - 2 * core

    loads = [
        pltpu.make_async_copy(src, dst, load_sem.at[i])
        for i, (src, dst) in enumerate(
            ((wg_hbm.at[0], wg), (wu_hbm.at[0], wu), (wd_hbm.at[0], wd), (proj_hbm, proj))
        )
    ]
    for load in loads:
        load.start()

    barrier = pltpu.get_barrier_semaphore()
    for k in range(1, n):
        pl.semaphore_signal(barrier, inc=1, device_id={"ep": lax.rem(me + k, n)})

    def block(section, pos):
        return pl.ds(pl.multiple_of(section * half + pos * rows, rows), rows)

    extra = x_all.shape[1] - feat
    lane = lax.broadcasted_iota(jnp.int32, (rows, extra), 1)
    expert_of = lax.rem(lane, n)
    weight = jnp.zeros((rows, extra), f32)
    ids = ids_ref[...]
    gates = gates_ref[...]
    for j in range(ids.shape[1]):
        weight = weight + jnp.where(ids[:, j : j + 1] == expert_of, gates[:, j : j + 1], 0.0)
    high = weight.astype(bf16).astype(f32)
    mid = (weight - high).astype(bf16).astype(f32)
    low = weight - high - mid
    coded = jnp.where(lane < n, high, jnp.where(lane < 2 * n, mid, jnp.where(lane < 3 * n, low, 0.0)))
    x_all[block(0, z), :feat] = rows_ref[...]
    x_all[block(0, z), feat:] = coded.astype(bf16)

    pl.semaphore_wait(barrier, n - 1)

    def remote(src, dst, send, recv, peer):
        return pltpu.make_async_remote_copy(
            src_ref=src, dst_ref=dst, send_sem=send, recv_sem=recv, device_id={"ep": peer}
        )

    def z_copy(k):
        here = x_all.at[block(0, z)]
        peer = lax.rem(z + k, line) * 4 + within
        return remote(here, here, gz_send.at[k], gz_recv.at[k], peer)

    def source(k):
        return lax.rem(z + line - k, line)

    def y_copy(k):
        return remote(
            x_all.at[block(0, source(k))],
            x_all.at[block(1, source(k))],
            gy_send.at[k],
            gy_recv.at[k],
            y_peer,
        )

    def s_copy(section, k):
        return remote(
            x_all.at[block(section, source(k))],
            x_all.at[block(2 + section, source(k))],
            gs_send.at[section, k],
            gs_recv.at[section, k],
            sibling,
        )

    gather_z = [z_copy(k) for k in range(1, line)]
    gather_y = [y_copy(k) for k in range(line)]
    gather_s = [[s_copy(section, k) for k in range(line)] for section in range(2)]
    for copy in gather_z:
        copy.start()
    gather_y[0].start()
    gather_s[0][0].start()
    gather_y[0].wait_recv()
    gather_s[1][0].start()
    for k in range(1, line):
        gather_z[k - 1].wait_recv()
        gather_y[k].start()
        gather_s[0][k].start()
    for k in range(1, line):
        gather_y[k].wait_recv()
        gather_s[1][k].start()

    loads[0].wait()
    loads[1].wait()

    def up_pass(base):
        span = pl.ds(base, 2 * half)

        def step(j, carry):
            cols = pl.ds(pl.multiple_of(j * tile, tile), tile)
            x = x_all[span, :feat]
            gate_act = jnp.dot(x, wg[:, cols], preferred_element_type=f32)
            up_act = jnp.dot(x, wu[:, cols], preferred_element_type=f32)
            inner[span, cols] = (jax.nn.silu(gate_act) * up_act).astype(bf16)
            return carry

        lax.fori_loop(0, hid // tile, step, 0)

    def down_pass(base):
        span = pl.ds(base, 2 * half)
        lanes = lax.broadcasted_iota(jnp.int32, (2 * half, extra), 1)
        mine = (lax.rem(lanes, n) == me) & (lanes < 3 * n)
        coef = jnp.sum(
            jnp.where(mine, x_all[span, feat:].astype(f32), 0.0), axis=1, keepdims=True
        )

        def step(j, carry):
            cols = pl.ds(pl.multiple_of(j * tile, tile), tile)
            out = jnp.dot(inner[span, :], wd[:, cols], preferred_element_type=f32)
            part[span, cols] = (out * coef).astype(bf16)
            return carry

        lax.fori_loop(0, feat // tile, step, 0)

    up_pass(0)
    for section in range(2):
        for k in range(line):
            gather_s[section][k].wait_recv()
    up_pass(2 * half)
    loads[2].wait()
    down_pass(2 * half)

    reduce_s = [
        remote(
            part.at[pl.ds((2 + section) * half, half)],
            sib_in.at[pl.ds(section * half, half)],
            rs_send.at[section],
            rs_recv.at[section],
            sibling,
        )
        for section in range(2)
    ]
    reduce_s[1].start()
    reduce_s[0].start()
    down_pass(0)

    def target(k):
        return lax.rem(z + k, line)

    reduce_y = [
        remote(
            pair_out.at[block(0, target(k))],
            y_in.at[block(0, target(k))],
            ry_send.at[k],
            ry_recv.at[k],
            y_peer,
        )
        for k in range(line)
    ]
    reduce_z = [
        remote(
            y_out.at[block(0, target(k))],
            z_in.at[block(0, k)],
            rz_send.at[k],
            rz_recv.at[k],
            target(k) * 4 + within,
        )
        for k in range(1, line)
    ]
    order = list(range(1, line)) + [0]
    reduce_s[1].wait_recv()
    for k in order:
        far = block(1, target(k))
        pair_out[block(0, target(k)), :] = (
            part[far, :].astype(f32) + sib_in[far, :].astype(f32)
        ).astype(bf16)
        reduce_y[k].start()
    reduce_s[0].wait_recv()
    for k in range(1, line):
        here = block(0, target(k))
        reduce_y[k].wait_recv()
        y_out[here, :] = (
            part[here, :].astype(f32) + sib_in[here, :].astype(f32) + y_in[here, :].astype(f32)
        ).astype(bf16)
        reduce_z[k - 1].start()
    here = block(0, z)
    reduce_y[0].wait_recv()
    total = (
        rows_ref[...].astype(f32)
        + part[here, :].astype(f32)
        + sib_in[here, :].astype(f32)
        + y_in[here, :].astype(f32)
    )
    for k in range(1, line):
        reduce_z[k - 1].wait_recv()
        total = total + z_in[k * rows : (k + 1) * rows, :].astype(f32)
    hidden = total.astype(bf16).astype(f32)
    scale = lax.rsqrt(jnp.mean(hidden * hidden, axis=-1, keepdims=True) + 1e-06)
    normed = (hidden * scale).astype(bf16)

    owner = lax.broadcasted_iota(jnp.int32, (n, rows), 0)
    pick = jnp.where(owner == slot_ref[...], 1.0, 0.0).astype(bf16)
    loads[3].wait()
    for j in range(width // tile):
        talk = jnp.dot(
            normed, proj[:, j * tile : (j + 1) * tile], preferred_element_type=f32
        ).astype(bf16)
        ordered = jnp.dot(pick, talk, preferred_element_type=f32)
        for i in range(tile // LANES):
            row_out[:, j * (tile // LANES) + i, :] = ordered[:, i * LANES : (i + 1) * LANES]
    exchange = []
    for k in range(1, n):
        peer = lax.rem(me + k, n)
        exchange.append(
            remote(row_out.at[peer], row_in.at[me], t_send.at[k], t_recv.at[k], peer)
        )
    for copy in exchange:
        copy.start()
    row_in[pl.ds(me, 1)] = row_out[pl.ds(me, 1)]
    for copy in exchange:
        copy.wait_recv()
    for i in range(width // LANES):
        owned_ref[:, i * LANES : (i + 1) * LANES] = row_in[:, i, :]

    for copy in (
        gather_z + gather_y + gather_s[0] + gather_s[1] + reduce_s + reduce_y + reduce_z + exchange
    ):
        copy.wait_send()


def dense_path(
    thinker_rows, expert_ids, gate_weights, w_gate, w_up, w_down, talker_proj, talker_slot
):
    n = lax.axis_size("ep")
    rows, feat = thinker_rows.shape
    hid = w_gate.shape[2]
    width = talker_proj.shape[1]
    line = n // 4
    every = n * rows
    extra = -(-3 * n // LANES) * LANES
    bf16, f32 = jnp.bfloat16, jnp.float32
    vmem = pl.BlockSpec(memory_space=pltpu.VMEM)
    hbm = pl.BlockSpec(memory_space=pl.ANY)
    dma = pltpu.SemaphoreType.DMA
    return pl.pallas_call(
        functools.partial(dense_kernel, n),
        out_shape=jax.ShapeDtypeStruct((rows, width), f32),
        in_specs=[vmem] * 4 + [hbm] * 4,
        out_specs=vmem,
        scratch_shapes=[
            pltpu.VMEM((feat, hid), bf16),
            pltpu.VMEM((feat, hid), bf16),
            pltpu.VMEM((hid, feat), bf16),
            pltpu.VMEM((feat, width), bf16),
            pltpu.VMEM((every, feat + extra), bf16),
            pltpu.VMEM((every, hid), bf16),
            pltpu.VMEM((every, feat), bf16),
            pltpu.VMEM((every // 2, feat), bf16),
            pltpu.VMEM((line * rows, feat), bf16),
            pltpu.VMEM((line * rows, feat), bf16),
            pltpu.VMEM((line * rows, feat), bf16),
            pltpu.VMEM((line * rows, feat), bf16),
            pltpu.VMEM((n, width // LANES, LANES), f32),
            pltpu.VMEM((n, width // LANES, LANES), f32),
            dma((4,)),
            dma((line,)),
            dma((line,)),
            dma((line,)),
            dma((line,)),
            dma((2, line)),
            dma((2, line)),
            dma((2,)),
            dma((2,)),
            dma((line,)),
            dma((line,)),
            dma((line,)),
            dma((line,)),
            dma((n,)),
            dma((n,)),
        ],
        compiler_params=pltpu.CompilerParams(
            collective_id=0, has_side_effects=True, vmem_limit_bytes=48 * 1024 * 1024
        ),
    )(thinker_rows, expert_ids, gate_weights, talker_slot, w_gate, w_up, w_down, talker_proj)


def local(
    thinker_rows,
    expert_ids,
    gate_weights,
    w_gate,
    w_up,
    w_down,
    talker_proj,
    talker_slot,
    speech_count,
    left_context,
    frame_offset,
    conv_weight,
):
    devices = lax.axis_size("ep")
    streams_here = thinker_rows.shape[0]
    dense = streams_here <= CAP and streams_here == devices and devices % 4 == 0
    path = dense_path if dense else capacity_path
    owned = path(
        thinker_rows, expert_ids, gate_weights, w_gate, w_up, w_down, talker_proj, talker_slot
    )
    return vocode(owned, speech_count, left_context, frame_offset, conv_weight)


def solution(mesh):
    in_specs = (
        P(("groups", "ep"), None),
        P(("groups", "ep"), None),
        P(("groups", "ep"), None),
        P("ep", None, None),
        P("ep", None, None),
        P("ep", None, None),
        P(),
        P(("groups", "ep"), None),
        P(("groups", "ep")),
        P(("groups", "ep"), None, None),
        P(),
        P(),
    )
    out_specs = P(("groups", "ep"), None, None)
    return jax.shard_map(local, mesh=mesh, in_specs=in_specs, out_specs=out_specs, check_vma=False)
```

```python
import functools

import jax
import jax.numpy as jnp
from jax import lax
from jax.experimental import pallas as pl
from jax.experimental.pallas import tpu as pltpu
from jax.sharding import PartitionSpec as P

CAP = 16
LANES = 128


def expert_block(block_rows, gate_mat, up_mat, down_mat):
    gate_act = jnp.dot(block_rows, gate_mat, preferred_element_type=jnp.float32)
    up_act = jnp.dot(block_rows, up_mat, preferred_element_type=jnp.float32)
    inner = (jax.nn.silu(gate_act) * up_act).astype(jnp.bfloat16)
    return jnp.dot(inner, down_mat, preferred_element_type=jnp.float32).astype(jnp.bfloat16)


def project(hidden, talker_proj):
    values = hidden.astype(jnp.float32)
    scaled = values * lax.rsqrt(jnp.mean(values * values, axis=-1, keepdims=True) + 1e-06)
    return jnp.dot(
        scaled.astype(jnp.bfloat16), talker_proj, preferred_element_type=jnp.float32
    ).astype(jnp.bfloat16)


def vocode(owned, speech_count, left_context, frame_offset, conv_weight):
    frames = owned.astype(jnp.float32)[:, None, :] + frame_offset[None, :, :]
    sequence = jnp.concatenate([left_context.astype(jnp.float32), frames], axis=1)
    taps = conv_weight.shape[0]
    horizon = frame_offset.shape[0]
    result = jnp.zeros_like(frames)
    for offset in range(taps):
        result = (
            result + conv_weight[offset][None, None, :] * sequence[:, offset : offset + horizon, :]
        )
    active = jnp.arange(horizon, dtype=jnp.int32)[None, :, None] < speech_count[:, None, None]
    return jnp.where(active, result, 0.0).astype(jnp.bfloat16)


def slot_positions(expert_ids, experts):
    flat_expert = expert_ids.reshape(-1)
    onehot = (flat_expert[:, None] == jnp.arange(experts, dtype=jnp.int32)[None, :]).astype(
        jnp.int32
    )
    position = jnp.sum((jnp.cumsum(onehot, axis=0) - onehot) * onehot, axis=1)
    return (flat_expert, position)


def run_and_return(buffer, w_gate, w_up, w_down):
    sources, slot_count, features = buffer.shape
    flattened = buffer.reshape(sources * slot_count, features)
    outputs = expert_block(flattened, w_gate[0], w_up[0], w_down[0]).reshape(
        sources, slot_count, features
    )
    return lax.all_to_all(outputs, "ep", split_axis=0, concat_axis=0, tiled=True)


def capacity_path(
    thinker_rows, expert_ids, gate_weights, w_gate, w_up, w_down, talker_proj, talker_slot
):
    devices = lax.axis_size("ep")
    streams_here, features = thinker_rows.shape
    chosen = expert_ids.shape[1]
    flat_expert, position = slot_positions(expert_ids, devices)
    row_index = jnp.arange(streams_here * chosen, dtype=jnp.int32) // chosen
    outgoing = (
        jnp.zeros((devices, CAP, features), jnp.bfloat16)
        .at[flat_expert, position]
        .set(thinker_rows[row_index])
    )
    returned = run_and_return(
        lax.all_to_all(outgoing, "ep", split_axis=0, concat_axis=0, tiled=True),
        w_gate,
        w_up,
        w_down,
    )
    lookup = (
        returned[flat_expert, position].astype(jnp.float32).reshape(streams_here, chosen, features)
    )
    mixture = jnp.sum(gate_weights[:, :, None] * lookup, axis=1)
    hidden = (thinker_rows.astype(jnp.float32) + mixture).astype(jnp.bfloat16)
    slots = talker_slot[0]
    per_owner = streams_here // devices
    talker_rows = project(hidden, talker_proj)
    placed = (
        jnp.zeros_like(talker_rows)
        .at[slots]
        .set(talker_rows)
        .reshape(devices, per_owner, talker_rows.shape[1])
    )
    return lax.all_to_all(placed, "ep", split_axis=0, concat_axis=0, tiled=True).reshape(
        streams_here, talker_rows.shape[1]
    )


def dense_kernel(
    n,
    rows_hbm,
    ids_hbm,
    gates_hbm,
    slot_hbm,
    count_hbm,
    context_hbm,
    offset_hbm,
    taps_hbm,
    wg_hbm,
    wu_hbm,
    wd_hbm,
    proj_hbm,
    voice_ref,
    ids_ref,
    gates_ref,
    slot_ref,
    count_ref,
    context,
    frame_offset,
    taps,
    base_voice,
    wg,
    wu,
    wd,
    proj,
    x_all,
    inner,
    part,
    sib_in,
    pair_out,
    y_in,
    y_out,
    z_in,
    row_out,
    row_in,
    load_sem,
    gz_send,
    gz_recv,
    gy_send,
    gy_recv,
    gs_send,
    gs_recv,
    rs_send,
    rs_recv,
    ry_send,
    ry_recv,
    rz_send,
    rz_recv,
    t_send,
    t_recv,
):
    f32, bf16 = jnp.float32, jnp.bfloat16
    rows, feat = rows_hbm.shape
    hid = wg.shape[1]
    width = proj.shape[1]
    line = n // 4
    half = line * rows
    tile = min(256, hid)
    me = lax.axis_index("ep")
    z = me // 4
    within = me % 4
    y = within // 2
    core = within % 2
    y_peer = me + 2 - 4 * y
    sibling = me + 1 - 2 * core

    def block(section, pos):
        return pl.ds(pl.multiple_of(section * half + pos * rows, rows), rows)

    own = block(0, z)
    loads = [
        pltpu.make_async_copy(src, dst, load_sem.at[i])
        for i, (src, dst) in enumerate(
            (
                (rows_hbm, x_all.at[own, pl.ds(0, feat)]),
                (ids_hbm, ids_ref),
                (gates_hbm, gates_ref),
                (slot_hbm, slot_ref),
                (count_hbm, count_ref),
                (context_hbm, context),
                (offset_hbm, frame_offset),
                (taps_hbm, taps),
                (wg_hbm.at[0], wg),
                (wu_hbm.at[0], wu),
                (wd_hbm.at[0], wd),
                (proj_hbm, proj),
            )
        )
    ]
    for load in loads:
        load.start()

    barrier = pltpu.get_barrier_semaphore()
    for k in range(1, n):
        pl.semaphore_signal(barrier, inc=1, device_id={"ep": lax.rem(me + k, n)})

    extra = x_all.shape[1] - feat
    spot = lax.broadcasted_iota(jnp.int32, (extra, rows), 0)
    expert_of = lax.rem(spot, n)
    weight = jnp.zeros((extra, rows), f32)
    for load in loads[:5]:
        load.wait()
    for j in range(ids_ref.shape[0]):
        weight = weight + jnp.where(
            ids_ref[j : j + 1, :] == expert_of, gates_ref[j : j + 1, :], 0.0
        )
    high = weight.astype(bf16).astype(f32)
    mid = (weight - high).astype(bf16).astype(f32)
    low = weight - high - mid
    coded = jnp.where(spot < n, high, jnp.where(spot < 2 * n, mid, jnp.where(spot < 3 * n, low, 0.0)))
    diagonal = lax.broadcasted_iota(jnp.int32, (rows, rows), 0) == lax.broadcasted_iota(
        jnp.int32, (rows, rows), 1
    )
    x_all[own, feat:] = lax.dot_general(
        jnp.where(diagonal, 1.0, 0.0).astype(bf16),
        coded.astype(bf16),
        (((1,), (1,)), ((), ())),
        preferred_element_type=f32,
    ).astype(bf16)

    pl.semaphore_wait(barrier, n - 1)

    def remote(src, dst, send, recv, peer):
        return pltpu.make_async_remote_copy(
            src_ref=src, dst_ref=dst, send_sem=send, recv_sem=recv, device_id={"ep": peer}
        )

    def z_copy(k):
        here = x_all.at[block(0, z)]
        peer = lax.rem(z + k, line) * 4 + within
        return remote(here, here, gz_send.at[k], gz_recv.at[k], peer)

    def source(k):
        return lax.rem(z + line - k, line)

    def y_copy(k):
        return remote(
            x_all.at[block(0, source(k))],
            x_all.at[block(1, source(k))],
            gy_send.at[k],
            gy_recv.at[k],
            y_peer,
        )

    def s_copy(section, k):
        return remote(
            x_all.at[block(section, source(k))],
            x_all.at[block(2 + section, source(k))],
            gs_send.at[section, k],
            gs_recv.at[section, k],
            sibling,
        )

    gather_z = [z_copy(k) for k in range(1, line)]
    gather_y = [y_copy(k) for k in range(line)]
    gather_s = [[s_copy(section, k) for k in range(line)] for section in range(2)]
    for copy in gather_z:
        copy.start()
    gather_y[0].start()
    gather_s[0][0].start()

    for load in loads[5:8]:
        load.wait()
    before = context.shape[0]
    horizon = frame_offset.shape[0]
    for f in range(horizon):
        voice = jnp.zeros((rows, width), f32)
        for t in range(taps.shape[0]):
            tap = taps[t : t + 1, :]
            if f + t < before:
                voice = voice + tap * context[f + t].astype(f32)
            else:
                voice = voice + tap * frame_offset[f + t - before : f + t - before + 1, :]
        base_voice[f] = voice

    gather_y[0].wait_recv()
    gather_s[1][0].start()
    for k in range(1, line):
        gather_z[k - 1].wait_recv()
        gather_y[k].start()
        gather_s[0][k].start()
    for k in range(1, line):
        gather_y[k].wait_recv()
        gather_s[1][k].start()

    loads[8].wait()
    loads[9].wait()

    def up_pass(base):
        span = pl.ds(base, 2 * half)

        def step(j, carry):
            cols = pl.ds(pl.multiple_of(j * tile, tile), tile)
            x = x_all[span, :feat]
            gate_act = jnp.dot(x, wg[:, cols], preferred_element_type=f32)
            up_act = jnp.dot(x, wu[:, cols], preferred_element_type=f32)
            inner[span, cols] = (jax.nn.silu(gate_act) * up_act).astype(bf16)
            return carry

        lax.fori_loop(0, hid // tile, step, 0)

    def down_pass(base):
        span = pl.ds(base, 2 * half)
        lanes = lax.broadcasted_iota(jnp.int32, (2 * half, extra), 1)
        mine = (lax.rem(lanes, n) == me) & (lanes < 3 * n)
        coef = jnp.sum(
            jnp.where(mine, x_all[span, feat:].astype(f32), 0.0), axis=1, keepdims=True
        )

        def step(j, carry):
            cols = pl.ds(pl.multiple_of(j * tile, tile), tile)
            out = jnp.dot(inner[span, :], wd[:, cols], preferred_element_type=f32)
            part[span, cols] = (out * coef).astype(bf16)
            return carry

        lax.fori_loop(0, feat // tile, step, 0)

    up_pass(0)
    for section in range(2):
        for k in range(line):
            gather_s[section][k].wait_recv()
    up_pass(2 * half)
    loads[10].wait()
    down_pass(2 * half)

    reduce_s = [
        remote(
            part.at[pl.ds((2 + section) * half, half)],
            sib_in.at[pl.ds(section * half, half)],
            rs_send.at[section],
            rs_recv.at[section],
            sibling,
        )
        for section in range(2)
    ]
    reduce_s[1].start()
    reduce_s[0].start()
    down_pass(0)

    def target(k):
        return lax.rem(z + k, line)

    reduce_y = [
        remote(
            pair_out.at[block(0, target(k))],
            y_in.at[block(0, target(k))],
            ry_send.at[k],
            ry_recv.at[k],
            y_peer,
        )
        for k in range(line)
    ]
    reduce_z = [
        remote(
            y_out.at[block(0, target(k))],
            z_in.at[block(0, k)],
            rz_send.at[k],
            rz_recv.at[k],
            target(k) * 4 + within,
        )
        for k in range(1, line)
    ]
    order = list(range(1, line)) + [0]
    reduce_s[1].wait_recv()
    for k in order:
        far = block(1, target(k))
        pair_out[block(0, target(k)), :] = (
            part[far, :].astype(f32) + sib_in[far, :].astype(f32)
        ).astype(bf16)
        reduce_y[k].start()
    reduce_s[0].wait_recv()
    for k in range(1, line):
        here = block(0, target(k))
        reduce_y[k].wait_recv()
        y_out[here, :] = (
            part[here, :].astype(f32) + sib_in[here, :].astype(f32) + y_in[here, :].astype(f32)
        ).astype(bf16)
        reduce_z[k - 1].start()
    here = block(0, z)
    reduce_y[0].wait_recv()
    total = (
        x_all[own, :feat].astype(f32)
        + part[here, :].astype(f32)
        + sib_in[here, :].astype(f32)
        + y_in[here, :].astype(f32)
    )
    for k in range(1, line):
        reduce_z[k - 1].wait_recv()
        total = total + z_in[k * rows : (k + 1) * rows, :].astype(f32)
    hidden = total.astype(bf16).astype(f32)
    scale = lax.rsqrt(jnp.mean(hidden * hidden, axis=-1, keepdims=True) + 1e-06)
    normed = (hidden * scale).astype(bf16)

    owner = lax.broadcasted_iota(jnp.int32, (n, rows), 0)
    pick = jnp.where(owner == slot_ref[...], 1.0, 0.0).astype(bf16)
    loads[11].wait()
    for j in range(width // tile):
        talk = jnp.dot(
            normed, proj[:, j * tile : (j + 1) * tile], preferred_element_type=f32
        ).astype(bf16)
        ordered = jnp.dot(pick, talk, preferred_element_type=f32)
        for i in range(tile // LANES):
            row_out[:, j * (tile // LANES) + i, :] = ordered[:, i * LANES : (i + 1) * LANES]
    exchange = []
    for k in range(1, n):
        peer = lax.rem(me + k, n)
        exchange.append(
            remote(row_out.at[peer], row_in.at[me], t_send.at[k], t_recv.at[k], peer)
        )
    for copy in exchange:
        copy.start()
    row_in[pl.ds(me, 1)] = row_out[pl.ds(me, 1)]
    for copy in exchange:
        copy.wait_recv()
    count = jnp.sum(
        jnp.where(diagonal, count_ref[...].astype(f32), 0.0), axis=1, keepdims=True
    )
    for i in range(width // LANES):
        cols = slice(i * LANES, (i + 1) * LANES)
        owned = row_in[:, i, :]
        for f in range(horizon):
            gain = jnp.sum(taps[before - f :, cols], axis=0, keepdims=True)
            voice = base_voice[f, :, cols] + gain * owned
            voice_ref[f, :, cols] = jnp.where(count > f, voice, 0.0).astype(bf16)

    for copy in (
        gather_z + gather_y + gather_s[0] + gather_s[1] + reduce_s + reduce_y + reduce_z + exchange
    ):
        copy.wait_send()


def dense_path(
    thinker_rows,
    expert_ids,
    gate_weights,
    w_gate,
    w_up,
    w_down,
    talker_proj,
    talker_slot,
    speech_count,
    left_context,
    frame_offset,
    conv_weight,
):
    n = lax.axis_size("ep")
    rows, feat = thinker_rows.shape
    hid = w_gate.shape[2]
    width = talker_proj.shape[1]
    line = n // 4
    every = n * rows
    extra = -(-3 * n // LANES) * LANES
    bf16, f32 = jnp.bfloat16, jnp.float32
    chosen = expert_ids.shape[1]
    before = left_context.shape[1]
    horizon = frame_offset.shape[0]
    vmem = pl.BlockSpec(memory_space=pltpu.VMEM)
    hbm = pl.BlockSpec(memory_space=pl.ANY)
    dma = pltpu.SemaphoreType.DMA
    voice = pl.pallas_call(
        functools.partial(dense_kernel, n),
        out_shape=jax.ShapeDtypeStruct((horizon, rows, width), bf16),
        in_specs=[hbm] * 12,
        out_specs=vmem,
        scratch_shapes=[
            pltpu.VMEM((chosen, rows), jnp.int32),
            pltpu.VMEM((chosen, rows), f32),
            pltpu.VMEM((1, rows), jnp.int32),
            pltpu.VMEM((1, rows), jnp.int32),
            pltpu.VMEM((before, rows, width), bf16),
            pltpu.VMEM((horizon, width), f32),
            pltpu.VMEM(conv_weight.shape, f32),
            pltpu.VMEM((horizon, rows, width), f32),
            pltpu.VMEM((feat, hid), bf16),
            pltpu.VMEM((feat, hid), bf16),
            pltpu.VMEM((hid, feat), bf16),
            pltpu.VMEM((feat, width), bf16),
            pltpu.VMEM((every, feat + extra), bf16),
            pltpu.VMEM((every, hid), bf16),
            pltpu.VMEM((every, feat), bf16),
            pltpu.VMEM((every // 2, feat), bf16),
            pltpu.VMEM((line * rows, feat), bf16),
            pltpu.VMEM((line * rows, feat), bf16),
            pltpu.VMEM((line * rows, feat), bf16),
            pltpu.VMEM((line * rows, feat), bf16),
            pltpu.VMEM((n, width // LANES, LANES), f32),
            pltpu.VMEM((n, width // LANES, LANES), f32),
            dma((12,)),
            dma((line,)),
            dma((line,)),
            dma((line,)),
            dma((line,)),
            dma((2, line)),
            dma((2, line)),
            dma((2,)),
            dma((2,)),
            dma((line,)),
            dma((line,)),
            dma((line,)),
            dma((line,)),
            dma((n,)),
            dma((n,)),
        ],
        compiler_params=pltpu.CompilerParams(
            collective_id=0, has_side_effects=True, vmem_limit_bytes=60 * 1024 * 1024
        ),
    )(
        thinker_rows,
        expert_ids.T,
        gate_weights.T,
        talker_slot,
        speech_count.reshape(1, rows),
        left_context.transpose(1, 0, 2),
        frame_offset,
        conv_weight,
        w_gate,
        w_up,
        w_down,
        talker_proj,
    )
    return voice.transpose(1, 0, 2)


def local(
    thinker_rows,
    expert_ids,
    gate_weights,
    w_gate,
    w_up,
    w_down,
    talker_proj,
    talker_slot,
    speech_count,
    left_context,
    frame_offset,
    conv_weight,
):
    devices = lax.axis_size("ep")
    streams_here = thinker_rows.shape[0]
    dense = streams_here <= CAP and streams_here == devices and devices % 4 == 0
    experts = (
        thinker_rows, expert_ids, gate_weights, w_gate, w_up, w_down, talker_proj, talker_slot
    )
    voices = (speech_count, left_context, frame_offset, conv_weight)
    if dense:
        return dense_path(*experts, *voices)
    return vocode(capacity_path(*experts), *voices)


def solution(mesh):
    in_specs = (
        P(("groups", "ep"), None),
        P(("groups", "ep"), None),
        P(("groups", "ep"), None),
        P("ep", None, None),
        P("ep", None, None),
        P("ep", None, None),
        P(),
        P(("groups", "ep"), None),
        P(("groups", "ep")),
        P(("groups", "ep"), None, None),
        P(),
        P(),
    )
    out_specs = P(("groups", "ep"), None, None)
    return jax.shard_map(local, mesh=mesh, in_specs=in_specs, out_specs=out_specs, check_vma=False)
```

```python
import functools

import jax
import jax.numpy as jnp
from jax import lax
from jax.experimental import pallas as pl
from jax.experimental.pallas import tpu as pltpu
from jax.sharding import PartitionSpec as P

CAP = 16
LANES = 128


def expert_block(block_rows, gate_mat, up_mat, down_mat):
    gate_act = jnp.dot(block_rows, gate_mat, preferred_element_type=jnp.float32)
    up_act = jnp.dot(block_rows, up_mat, preferred_element_type=jnp.float32)
    inner = (jax.nn.silu(gate_act) * up_act).astype(jnp.bfloat16)
    return jnp.dot(inner, down_mat, preferred_element_type=jnp.float32).astype(jnp.bfloat16)


def project(hidden, talker_proj):
    values = hidden.astype(jnp.float32)
    scaled = values * lax.rsqrt(jnp.mean(values * values, axis=-1, keepdims=True) + 1e-06)
    return jnp.dot(
        scaled.astype(jnp.bfloat16), talker_proj, preferred_element_type=jnp.float32
    ).astype(jnp.bfloat16)


def vocode(owned, speech_count, left_context, frame_offset, conv_weight):
    frames = owned.astype(jnp.float32)[:, None, :] + frame_offset[None, :, :]
    sequence = jnp.concatenate([left_context.astype(jnp.float32), frames], axis=1)
    taps = conv_weight.shape[0]
    horizon = frame_offset.shape[0]
    result = jnp.zeros_like(frames)
    for offset in range(taps):
        result = (
            result + conv_weight[offset][None, None, :] * sequence[:, offset : offset + horizon, :]
        )
    active = jnp.arange(horizon, dtype=jnp.int32)[None, :, None] < speech_count[:, None, None]
    return jnp.where(active, result, 0.0).astype(jnp.bfloat16)


def slot_positions(expert_ids, experts):
    flat_expert = expert_ids.reshape(-1)
    onehot = (flat_expert[:, None] == jnp.arange(experts, dtype=jnp.int32)[None, :]).astype(
        jnp.int32
    )
    position = jnp.sum((jnp.cumsum(onehot, axis=0) - onehot) * onehot, axis=1)
    return (flat_expert, position)


def run_and_return(buffer, w_gate, w_up, w_down):
    sources, slot_count, features = buffer.shape
    flattened = buffer.reshape(sources * slot_count, features)
    outputs = expert_block(flattened, w_gate[0], w_up[0], w_down[0]).reshape(
        sources, slot_count, features
    )
    return lax.all_to_all(outputs, "ep", split_axis=0, concat_axis=0, tiled=True)


def capacity_path(
    thinker_rows, expert_ids, gate_weights, w_gate, w_up, w_down, talker_proj, talker_slot
):
    devices = lax.axis_size("ep")
    streams_here, features = thinker_rows.shape
    chosen = expert_ids.shape[1]
    flat_expert, position = slot_positions(expert_ids, devices)
    row_index = jnp.arange(streams_here * chosen, dtype=jnp.int32) // chosen
    outgoing = (
        jnp.zeros((devices, CAP, features), jnp.bfloat16)
        .at[flat_expert, position]
        .set(thinker_rows[row_index])
    )
    returned = run_and_return(
        lax.all_to_all(outgoing, "ep", split_axis=0, concat_axis=0, tiled=True),
        w_gate,
        w_up,
        w_down,
    )
    lookup = (
        returned[flat_expert, position].astype(jnp.float32).reshape(streams_here, chosen, features)
    )
    mixture = jnp.sum(gate_weights[:, :, None] * lookup, axis=1)
    hidden = (thinker_rows.astype(jnp.float32) + mixture).astype(jnp.bfloat16)
    slots = talker_slot[0]
    per_owner = streams_here // devices
    talker_rows = project(hidden, talker_proj)
    placed = (
        jnp.zeros_like(talker_rows)
        .at[slots]
        .set(talker_rows)
        .reshape(devices, per_owner, talker_rows.shape[1])
    )
    return lax.all_to_all(placed, "ep", split_axis=0, concat_axis=0, tiled=True).reshape(
        streams_here, talker_rows.shape[1]
    )


def dense_kernel(
    n,
    rows_hbm,
    ids_hbm,
    gates_hbm,
    slot_hbm,
    count_hbm,
    context_hbm,
    offset_hbm,
    taps_hbm,
    wg_hbm,
    wu_hbm,
    wd_hbm,
    proj_hbm,
    voice_ref,
    ids_ref,
    gates_ref,
    slot_ref,
    count_ref,
    context,
    frame_offset,
    taps,
    base_voice,
    wg,
    wu,
    wd,
    proj,
    x_all,
    inner,
    part,
    sib_in,
    pair_out,
    y_in,
    y_out,
    z_in,
    row_out,
    row_in,
    load_sem,
    gz_send,
    gz_recv,
    gy_send,
    gy_recv,
    gs_send,
    gs_recv,
    rs_send,
    rs_recv,
    ry_send,
    ry_recv,
    rz_send,
    rz_recv,
    t_send,
    t_recv,
):
    f32, bf16 = jnp.float32, jnp.bfloat16
    rows, feat = rows_hbm.shape
    hid = wg.shape[1]
    width = proj.shape[1]
    line = n // 4
    half = line * rows
    tile = min(256, hid)
    me = lax.axis_index("ep")
    z = me // 4
    within = me % 4
    y = within // 2
    core = within % 2
    y_peer = me + 2 - 4 * y
    sibling = me + 1 - 2 * core

    def block(section, pos):
        return pl.ds(pl.multiple_of(section * half + pos * rows, rows), rows)

    own = block(0, z)
    loads = [
        pltpu.make_async_copy(src, dst, load_sem.at[i])
        for i, (src, dst) in enumerate(
            (
                (rows_hbm, x_all.at[own, pl.ds(0, feat)]),
                (ids_hbm, ids_ref),
                (gates_hbm, gates_ref),
                (slot_hbm, slot_ref),
                (count_hbm, count_ref),
                (context_hbm, context),
                (offset_hbm, frame_offset),
                (taps_hbm, taps),
                (wg_hbm.at[0], wg),
                (wu_hbm.at[0], wu),
                (wd_hbm.at[0], wd),
                (proj_hbm, proj),
            )
        )
    ]
    for load in loads:
        load.start()

    barrier = pltpu.get_barrier_semaphore()
    for k in range(1, n):
        pl.semaphore_signal(barrier, inc=1, device_id={"ep": lax.rem(me + k, n)})

    extra = x_all.shape[1] - feat
    spot = lax.broadcasted_iota(jnp.int32, (extra, rows), 0)
    expert_of = lax.rem(spot, n)
    weight = jnp.zeros((extra, rows), f32)
    for load in loads[:5]:
        load.wait()
    for j in range(ids_ref.shape[0]):
        weight = weight + jnp.where(
            ids_ref[j : j + 1, :] == expert_of, gates_ref[j : j + 1, :], 0.0
        )
    high = weight.astype(bf16).astype(f32)
    mid = (weight - high).astype(bf16).astype(f32)
    low = weight - high - mid
    coded = jnp.where(spot < n, high, jnp.where(spot < 2 * n, mid, jnp.where(spot < 3 * n, low, 0.0)))
    diagonal = lax.broadcasted_iota(jnp.int32, (rows, rows), 0) == lax.broadcasted_iota(
        jnp.int32, (rows, rows), 1
    )
    x_all[own, feat:] = lax.dot_general(
        jnp.where(diagonal, 1.0, 0.0).astype(bf16),
        coded.astype(bf16),
        (((1,), (1,)), ((), ())),
        preferred_element_type=f32,
    ).astype(bf16)

    pl.semaphore_wait(barrier, n - 1)

    def remote(src, dst, send, recv, peer):
        return pltpu.make_async_remote_copy(
            src_ref=src, dst_ref=dst, send_sem=send, recv_sem=recv, device_id={"ep": peer}
        )

    def z_copy(up, src):
        here = x_all.at[block(0, src)]
        step = 4 if up else -4
        return remote(here, here, gz_send.at[int(up), src], gz_recv.at[src], me + step)

    def y_copy(src):
        return remote(
            x_all.at[block(0, src)],
            x_all.at[block(2, src)],
            gy_send.at[src],
            gy_recv.at[src],
            y_peer,
        )

    def s_copy(section, src):
        return remote(
            x_all.at[block(2 * section, src)],
            x_all.at[block(2 * section + 1, src)],
            gs_send.at[section, src],
            gs_recv.at[section, src],
            sibling,
        )

    def at_distance(d, use):
        for src in (z,) if d == 0 else (z - d, z + d):
            pl.when((src >= 0) & (src < line))(functools.partial(use, src))

    def pass_z(d, act):
        def go(up, src):
            pl.when((z + 1 < line) if up else (z > 0))(lambda: act(z_copy(up, src)))

        if d == 0:
            go(True, z)
            go(False, z)
        else:
            pl.when(z - d >= 0)(lambda: go(True, z - d))
            pl.when(z + d < line)(lambda: go(False, z + d))

    def from_z(d):
        at_distance(d, lambda src: z_copy(True, src).wait_recv())

    def hand_on(src):
        y_copy(src).start()
        s_copy(0, src).start()

    def from_y(src):
        y_copy(src).wait_recv()
        s_copy(1, src).start()

    pass_z(0, lambda copy: copy.start())
    hand_on(z)

    for load in loads[5:8]:
        load.wait()
    before = context.shape[0]
    horizon = frame_offset.shape[0]
    for f in range(horizon):
        voice = jnp.zeros((rows, width), f32)
        for t in range(taps.shape[0]):
            tap = taps[t : t + 1, :]
            if f + t < before:
                voice = voice + tap * context[f + t].astype(f32)
            else:
                voice = voice + tap * frame_offset[f + t - before : f + t - before + 1, :]
        base_voice[f] = voice

    for d in range(1, line):
        from_z(d)
        pass_z(d, lambda copy: copy.start())
        at_distance(d, hand_on)
        if d < line - 1:
            at_distance(d - 1, from_y)

    loads[8].wait()
    loads[9].wait()

    def up_pass(base):
        span = pl.ds(base, 2 * half)

        def step(j, carry):
            cols = pl.ds(pl.multiple_of(j * tile, tile), tile)
            x = x_all[span, :feat]
            gate_act = jnp.dot(x, wg[:, cols], preferred_element_type=f32)
            up_act = jnp.dot(x, wu[:, cols], preferred_element_type=f32)
            inner[span, cols] = (jax.nn.silu(gate_act) * up_act).astype(bf16)
            return carry

        lax.fori_loop(0, hid // tile, step, 0)

    def down_pass(base, cut):
        span = pl.ds(base, 2 * half)
        lanes = lax.broadcasted_iota(jnp.int32, (2 * half, extra), 1)
        mine = (lax.rem(lanes, n) == me) & (lanes < 3 * n)
        coef = jnp.sum(
            jnp.where(mine, x_all[span, feat:].astype(f32), 0.0), axis=1, keepdims=True
        )

        def step(j, carry):
            cols = pl.ds(pl.multiple_of(cut * piece + j * tile, tile), tile)
            out = jnp.dot(inner[span, :], wd[:, cols], preferred_element_type=f32)
            part[span, cols] = (out * coef).astype(bf16)
            return carry

        lax.fori_loop(0, piece // tile, step, 0)

    cuts = rs_send.shape[1]
    piece = feat // cuts

    def columns(cut):
        return pl.ds(cut * piece, piece)

    reduce_s = [
        [
            remote(
                part.at[pl.ds((2 * section + 1) * half, half), columns(cut)],
                sib_in.at[pl.ds(section * half, half), columns(cut)],
                rs_send.at[section, cut],
                rs_recv.at[section, cut],
                sibling,
            )
            for cut in range(cuts)
        ]
        for section in range(2)
    ]
    for src in range(line):
        s_copy(0, src).wait_recv()
    up_pass(0)
    for d in range(max(line - 2, 0), line):
        at_distance(d, from_y)
    loads[10].wait()
    for cut in range(cuts):
        down_pass(0, cut)
        reduce_s[0][cut].start()
    for src in range(line):
        s_copy(1, src).wait_recv()
    up_pass(2 * half)
    for cut in range(cuts):
        down_pass(2 * half, cut)
        reduce_s[1][cut].start()

    def target(k):
        return lax.rem(z + k, line)

    reduce_y = [
        [
            remote(
                pair_out.at[block(0, target(k)), columns(cut)],
                y_in.at[block(0, target(k)), columns(cut)],
                ry_send.at[k, cut],
                ry_recv.at[k, cut],
                y_peer,
            )
            for cut in range(cuts)
        ]
        for k in range(line)
    ]
    reduce_z = [
        [
            remote(
                y_out.at[block(0, target(k)), columns(cut)],
                z_in.at[block(0, k), columns(cut)],
                rz_send.at[k, cut],
                rz_recv.at[k, cut],
                target(k) * 4 + within,
            )
            for cut in range(cuts)
        ]
        for k in range(1, line)
    ]

    def to_y(k, cut):
        cols = columns(cut)
        mine, theirs = block(2, target(k)), block(1, target(k))
        pair_out[block(0, target(k)), cols] = (
            part[mine, cols].astype(f32) + sib_in[theirs, cols].astype(f32)
        ).astype(bf16)
        reduce_y[k][cut].start()

    for cut in range(cuts):
        reduce_s[1][cut].wait_recv()
        for k in range(1, line):
            to_y(k, cut)
    for cut in range(cuts):
        to_y(0, cut)
    for cut in range(cuts):
        cols = columns(cut)
        reduce_s[0][cut].wait_recv()
        for k in range(1, line):
            here = block(0, target(k))
            reduce_y[k][cut].wait_recv()
            y_out[here, cols] = (
                part[here, cols].astype(f32)
                + sib_in[here, cols].astype(f32)
                + y_in[here, cols].astype(f32)
            ).astype(bf16)
            reduce_z[k - 1][cut].start()
    for cut in range(cuts):
        reduce_y[0][cut].wait_recv()
    total = (
        x_all[own, :feat].astype(f32)
        + part[own, :].astype(f32)
        + sib_in[own, :].astype(f32)
        + y_in[own, :].astype(f32)
    )
    for k in range(1, line):
        for cut in range(cuts):
            reduce_z[k - 1][cut].wait_recv()
        total = total + z_in[k * rows : (k + 1) * rows, :].astype(f32)
    hidden = total.astype(bf16).astype(f32)
    scale = lax.rsqrt(jnp.mean(hidden * hidden, axis=-1, keepdims=True) + 1e-06)
    normed = (hidden * scale).astype(bf16)

    owner = lax.broadcasted_iota(jnp.int32, (n, rows), 0)
    pick = jnp.where(owner == slot_ref[...], 1.0, 0.0).astype(bf16)
    loads[11].wait()
    for j in range(width // tile):
        talk = jnp.dot(
            normed, proj[:, j * tile : (j + 1) * tile], preferred_element_type=f32
        ).astype(bf16)
        ordered = jnp.dot(pick, talk, preferred_element_type=f32)
        for i in range(tile // LANES):
            row_out[:, j * (tile // LANES) + i, :] = ordered[:, i * LANES : (i + 1) * LANES]
    exchange = []
    for k in range(1, n):
        peer = lax.rem(me + k, n)
        exchange.append(
            remote(row_out.at[peer], row_in.at[me], t_send.at[k], t_recv.at[k], peer)
        )
    for copy in exchange:
        copy.start()
    row_in[pl.ds(me, 1)] = row_out[pl.ds(me, 1)]
    for copy in exchange:
        copy.wait_recv()
    count = jnp.sum(
        jnp.where(diagonal, count_ref[...].astype(f32), 0.0), axis=1, keepdims=True
    )
    for i in range(width // LANES):
        cols = slice(i * LANES, (i + 1) * LANES)
        owned = row_in[:, i, :]
        for f in range(horizon):
            gain = jnp.sum(taps[before - f :, cols], axis=0, keepdims=True)
            voice = base_voice[f, :, cols] + gain * owned
            voice_ref[f, :, cols] = jnp.where(count > f, voice, 0.0).astype(bf16)

    for d in range(line):
        pass_z(d, lambda copy: copy.wait_send())
    for src in range(line):
        y_copy(src).wait_send()
        s_copy(0, src).wait_send()
        s_copy(1, src).wait_send()
    for group in reduce_s + reduce_y + reduce_z + [exchange]:
        for copy in group:
            copy.wait_send()


def dense_path(
    thinker_rows,
    expert_ids,
    gate_weights,
    w_gate,
    w_up,
    w_down,
    talker_proj,
    talker_slot,
    speech_count,
    left_context,
    frame_offset,
    conv_weight,
):
    n = lax.axis_size("ep")
    rows, feat = thinker_rows.shape
    hid = w_gate.shape[2]
    width = talker_proj.shape[1]
    line = n // 4
    every = n * rows
    extra = -(-3 * n // LANES) * LANES
    bf16, f32 = jnp.bfloat16, jnp.float32
    chosen = expert_ids.shape[1]
    before = left_context.shape[1]
    horizon = frame_offset.shape[0]
    cuts = 2
    vmem = pl.BlockSpec(memory_space=pltpu.VMEM)
    hbm = pl.BlockSpec(memory_space=pl.ANY)
    dma = pltpu.SemaphoreType.DMA
    voice = pl.pallas_call(
        functools.partial(dense_kernel, n),
        out_shape=jax.ShapeDtypeStruct((horizon, rows, width), bf16),
        in_specs=[hbm] * 12,
        out_specs=vmem,
        scratch_shapes=[
            pltpu.VMEM((chosen, rows), jnp.int32),
            pltpu.VMEM((chosen, rows), f32),
            pltpu.VMEM((1, rows), jnp.int32),
            pltpu.VMEM((1, rows), jnp.int32),
            pltpu.VMEM((before, rows, width), bf16),
            pltpu.VMEM((horizon, width), f32),
            pltpu.VMEM(conv_weight.shape, f32),
            pltpu.VMEM((horizon, rows, width), f32),
            pltpu.VMEM((feat, hid), bf16),
            pltpu.VMEM((feat, hid), bf16),
            pltpu.VMEM((hid, feat), bf16),
            pltpu.VMEM((feat, width), bf16),
            pltpu.VMEM((every, feat + extra), bf16),
            pltpu.VMEM((every, hid), bf16),
            pltpu.VMEM((every, feat), bf16),
            pltpu.VMEM((every // 2, feat), bf16),
            pltpu.VMEM((line * rows, feat), bf16),
            pltpu.VMEM((line * rows, feat), bf16),
            pltpu.VMEM((line * rows, feat), bf16),
            pltpu.VMEM((line * rows, feat), bf16),
            pltpu.VMEM((n, width // LANES, LANES), f32),
            pltpu.VMEM((n, width // LANES, LANES), f32),
            dma((12,)),
            dma((2, line)),
            dma((line,)),
            dma((line,)),
            dma((line,)),
            dma((2, line)),
            dma((2, line)),
            dma((2, cuts)),
            dma((2, cuts)),
            dma((line, cuts)),
            dma((line, cuts)),
            dma((line, cuts)),
            dma((line, cuts)),
            dma((n,)),
            dma((n,)),
        ],
        compiler_params=pltpu.CompilerParams(
            collective_id=0, has_side_effects=True, vmem_limit_bytes=60 * 1024 * 1024
        ),
    )(
        thinker_rows,
        expert_ids.T,
        gate_weights.T,
        talker_slot,
        speech_count.reshape(1, rows),
        left_context.transpose(1, 0, 2),
        frame_offset,
        conv_weight,
        w_gate,
        w_up,
        w_down,
        talker_proj,
    )
    return voice.transpose(1, 0, 2)


def local(
    thinker_rows,
    expert_ids,
    gate_weights,
    w_gate,
    w_up,
    w_down,
    talker_proj,
    talker_slot,
    speech_count,
    left_context,
    frame_offset,
    conv_weight,
):
    devices = lax.axis_size("ep")
    streams_here = thinker_rows.shape[0]
    dense = streams_here <= CAP and streams_here == devices and devices % 4 == 0
    experts = (
        thinker_rows, expert_ids, gate_weights, w_gate, w_up, w_down, talker_proj, talker_slot
    )
    voices = (speech_count, left_context, frame_offset, conv_weight)
    if dense:
        return dense_path(*experts, *voices)
    return vocode(capacity_path(*experts), *voices)


def solution(mesh):
    in_specs = (
        P(("groups", "ep"), None),
        P(("groups", "ep"), None),
        P(("groups", "ep"), None),
        P("ep", None, None),
        P("ep", None, None),
        P("ep", None, None),
        P(),
        P(("groups", "ep"), None),
        P(("groups", "ep")),
        P(("groups", "ep"), None, None),
        P(),
        P(),
    )
    out_specs = P(("groups", "ep"), None, None)
    return jax.shard_map(local, mesh=mesh, in_specs=in_specs, out_specs=out_specs, check_vma=False)
```

```python
import functools

import jax
import jax.numpy as jnp
from jax import lax
from jax.experimental import pallas as pl
from jax.experimental.pallas import tpu as pltpu
from jax.sharding import PartitionSpec as P

CAP = 16
LANES = 128


def expert_block(block_rows, gate_mat, up_mat, down_mat):
    gate_act = jnp.dot(block_rows, gate_mat, preferred_element_type=jnp.float32)
    up_act = jnp.dot(block_rows, up_mat, preferred_element_type=jnp.float32)
    inner = (jax.nn.silu(gate_act) * up_act).astype(jnp.bfloat16)
    return jnp.dot(inner, down_mat, preferred_element_type=jnp.float32).astype(jnp.bfloat16)


def project(hidden, talker_proj):
    values = hidden.astype(jnp.float32)
    scaled = values * lax.rsqrt(jnp.mean(values * values, axis=-1, keepdims=True) + 1e-06)
    return jnp.dot(
        scaled.astype(jnp.bfloat16), talker_proj, preferred_element_type=jnp.float32
    ).astype(jnp.bfloat16)


def vocode(owned, speech_count, left_context, frame_offset, conv_weight):
    frames = owned.astype(jnp.float32)[:, None, :] + frame_offset[None, :, :]
    sequence = jnp.concatenate([left_context.astype(jnp.float32), frames], axis=1)
    taps = conv_weight.shape[0]
    horizon = frame_offset.shape[0]
    result = jnp.zeros_like(frames)
    for offset in range(taps):
        result = (
            result + conv_weight[offset][None, None, :] * sequence[:, offset : offset + horizon, :]
        )
    active = jnp.arange(horizon, dtype=jnp.int32)[None, :, None] < speech_count[:, None, None]
    return jnp.where(active, result, 0.0).astype(jnp.bfloat16)


def slot_positions(expert_ids, experts):
    flat_expert = expert_ids.reshape(-1)
    onehot = (flat_expert[:, None] == jnp.arange(experts, dtype=jnp.int32)[None, :]).astype(
        jnp.int32
    )
    position = jnp.sum((jnp.cumsum(onehot, axis=0) - onehot) * onehot, axis=1)
    return (flat_expert, position)


def run_and_return(buffer, w_gate, w_up, w_down):
    sources, slot_count, features = buffer.shape
    flattened = buffer.reshape(sources * slot_count, features)
    outputs = expert_block(flattened, w_gate[0], w_up[0], w_down[0]).reshape(
        sources, slot_count, features
    )
    return lax.all_to_all(outputs, "ep", split_axis=0, concat_axis=0, tiled=True)


def capacity_path(
    thinker_rows, expert_ids, gate_weights, w_gate, w_up, w_down, talker_proj, talker_slot
):
    devices = lax.axis_size("ep")
    streams_here, features = thinker_rows.shape
    chosen = expert_ids.shape[1]
    flat_expert, position = slot_positions(expert_ids, devices)
    row_index = jnp.arange(streams_here * chosen, dtype=jnp.int32) // chosen
    outgoing = (
        jnp.zeros((devices, CAP, features), jnp.bfloat16)
        .at[flat_expert, position]
        .set(thinker_rows[row_index])
    )
    returned = run_and_return(
        lax.all_to_all(outgoing, "ep", split_axis=0, concat_axis=0, tiled=True),
        w_gate,
        w_up,
        w_down,
    )
    lookup = (
        returned[flat_expert, position].astype(jnp.float32).reshape(streams_here, chosen, features)
    )
    mixture = jnp.sum(gate_weights[:, :, None] * lookup, axis=1)
    hidden = (thinker_rows.astype(jnp.float32) + mixture).astype(jnp.bfloat16)
    slots = talker_slot[0]
    per_owner = streams_here // devices
    talker_rows = project(hidden, talker_proj)
    placed = (
        jnp.zeros_like(talker_rows)
        .at[slots]
        .set(talker_rows)
        .reshape(devices, per_owner, talker_rows.shape[1])
    )
    return lax.all_to_all(placed, "ep", split_axis=0, concat_axis=0, tiled=True).reshape(
        streams_here, talker_rows.shape[1]
    )


def dense_kernel(
    n,
    rows_hbm,
    ids_hbm,
    gates_hbm,
    slot_hbm,
    count_hbm,
    context_hbm,
    offset_hbm,
    taps_hbm,
    wg_hbm,
    wu_hbm,
    wd_hbm,
    proj_hbm,
    voice_ref,
    rows_ref,
    ids_ref,
    gates_ref,
    slot_ref,
    count_ref,
    context,
    frame_offset,
    taps,
    base_voice,
    wg,
    wu,
    wd,
    proj,
    x_all,
    inner,
    grouped,
    part,
    sib_in,
    pair_out,
    y_in,
    y_out,
    z_in,
    load_sem,
    gz_send,
    gz_recv,
    gy_send,
    gy_recv,
    gs_send,
    gs_recv,
    rs_send,
    rs_recv,
    ry_send,
    ry_recv,
    rz_send,
    rz_recv,
):
    f32, bf16 = jnp.float32, jnp.bfloat16
    rows, feat = rows_hbm.shape
    hid = wg.shape[1]
    width = proj.shape[1]
    line = n // 4
    half = line * rows
    tile = min(256, hid)
    me = lax.axis_index("ep")
    z = me // 4
    within = me % 4
    y = within // 2
    core = within % 2
    y_peer = me + 2 - 4 * y
    sibling = me + 1 - 2 * core

    def block(section, pos):
        return pl.ds(pl.multiple_of(section * half + pos * rows, rows), rows)

    own = block(0, z)
    loads = [
        pltpu.make_async_copy(src, dst, load_sem.at[i])
        for i, (src, dst) in enumerate(
            (
                (rows_hbm, rows_ref),
                (ids_hbm, ids_ref),
                (gates_hbm, gates_ref),
                (slot_hbm, slot_ref),
                (count_hbm, count_ref),
                (context_hbm, context),
                (offset_hbm, frame_offset),
                (taps_hbm, taps),
                (wg_hbm.at[0], wg),
                (wu_hbm.at[0], wu),
                (wd_hbm.at[0], wd),
                (proj_hbm, proj),
            )
        )
    ]
    for load in loads[:4]:
        load.start()

    z_peers = [lax.rem(z + k, line) * 4 + within for k in range(1, line)]
    partners = z_peers + [y_peer, sibling]
    barrier = pltpu.get_barrier_semaphore()
    for peer in partners:
        pl.semaphore_signal(barrier, inc=1, device_id={"ep": peer})

    extra = x_all.shape[1] - feat
    spot = lax.broadcasted_iota(jnp.int32, (extra, rows), 0)
    expert_of = lax.rem(spot, n)
    weight = jnp.zeros((extra, rows), f32)
    for load in loads[:4]:
        load.wait()
    for j in range(ids_ref.shape[0]):
        weight = weight + jnp.where(
            ids_ref[j : j + 1, :] == expert_of, gates_ref[j : j + 1, :], 0.0
        )
    high = weight.astype(bf16).astype(f32)
    mid = (weight - high).astype(bf16).astype(f32)
    low = weight - high - mid
    coded = jnp.where(spot < n, high, jnp.where(spot < 2 * n, mid, jnp.where(spot < 3 * n, low, 0.0)))
    owner = lax.broadcasted_iota(jnp.int32, (n, rows), 0)
    pick = jnp.where(owner == slot_ref[...], 1.0, 0.0).astype(bf16)
    x_all[own, :feat] = jnp.dot(pick, rows_ref[...], preferred_element_type=f32).astype(bf16)
    x_all[own, feat:] = lax.dot_general(
        pick, coded.astype(bf16), (((1,), (1,)), ((), ())), preferred_element_type=f32
    ).astype(bf16)

    pl.semaphore_wait(barrier, len(partners))

    def remote(src, dst, send, recv, peer):
        return pltpu.make_async_remote_copy(
            src_ref=src, dst_ref=dst, send_sem=send, recv_sem=recv, device_id={"ep": peer}
        )

    def z_copy(peer, src):
        here = x_all.at[block(0, src)]
        return remote(here, here, gz_send.at[peer], gz_recv.at[src], peer * 4 + within)

    def y_copy(src):
        return remote(
            x_all.at[block(0, src)],
            x_all.at[block(2, src)],
            gy_send.at[src],
            gy_recv.at[src],
            y_peer,
        )

    def s_copy(section, src):
        return remote(
            x_all.at[block(2 * section, src)],
            x_all.at[block(2 * section + 1, src)],
            gs_send.at[section, src],
            gs_recv.at[section, src],
            sibling,
        )

    def at_distance(d, use):
        for src in (z,) if d == 0 else (z - d, z + d):
            pl.when((src >= 0) & (src < line))(functools.partial(use, src))

    def to_z(d, act):
        at_distance(d, lambda peer: act(z_copy(peer, z)))

    def from_z(d):
        at_distance(d, lambda src: z_copy(src, src).wait_recv())

    def hand_on(src):
        y_copy(src).start()
        s_copy(0, src).start()

    def from_y(src):
        y_copy(src).wait_recv()
        s_copy(1, src).start()

    to_z(1, lambda copy: copy.start())
    hand_on(z)
    for d in range(2, line):
        to_z(d, lambda copy: copy.start())
    for load in loads[4:]:
        load.start()

    for load in loads[4:8]:
        load.wait()
    before = context.shape[0]
    horizon = frame_offset.shape[0]
    for f in range(horizon):
        voice = jnp.zeros((rows, width), f32)
        for t in range(taps.shape[0]):
            tap = taps[t : t + 1, :]
            if f + t < before:
                voice = voice + tap * context[f + t].astype(f32)
            else:
                voice = voice + tap * frame_offset[f + t - before : f + t - before + 1, :]
        base_voice[f] = voice

    for d in range(1, line):
        from_z(d)
        at_distance(d, hand_on)
        if d < line - 1:
            at_distance(d - 1, from_y)

    loads[8].wait()
    loads[9].wait()

    def up_pass(base):
        span = pl.ds(base, 2 * half)
        lanes = lax.broadcasted_iota(jnp.int32, (2 * half, extra), 1)
        mine = (lax.rem(lanes, n) == me) & (lanes < 3 * n)
        coef = jnp.sum(
            jnp.where(mine, x_all[span, feat:].astype(f32), 0.0), axis=1, keepdims=True
        )

        def step(j, carry):
            cols = pl.ds(pl.multiple_of(j * tile, tile), tile)
            x = x_all[span, :feat]
            gate_act = jnp.dot(x, wg[:, cols], preferred_element_type=f32)
            up_act = jnp.dot(x, wu[:, cols], preferred_element_type=f32)
            inner[span, cols] = (jax.nn.silu(gate_act) * up_act * coef).astype(bf16)
            return carry

        lax.fori_loop(0, hid // tile, step, 0)

    def place(index):
        section = index // half
        device = (
            (index % half) // rows * 4
            + jnp.where(section // 2 == 0, y, 1 - y) * 2
            + jnp.where(section % 2 == 0, core, 1 - core)
        )
        return device, index % rows

    def regroup():
        every = n * rows
        row_owner, row_source = place(lax.broadcasted_iota(jnp.int32, (every, 1), 0))
        col_source, col_owner = place(lax.broadcasted_iota(jnp.int32, (1, every), 1))
        match = (row_owner == col_owner) & (row_source == col_source)
        return jnp.where(match, 1.0, 0.0).astype(bf16)

    def down_pass(base, cut):
        span = pl.ds(base, 2 * half)

        def step(j, carry):
            cols = pl.ds(pl.multiple_of(cut * piece + j * tile, tile), tile)
            out = jnp.dot(grouped[span, :], wd[:, cols], preferred_element_type=f32)
            part[span, cols] = out.astype(bf16)
            return carry

        lax.fori_loop(0, piece // tile, step, 0)

    cuts = rs_send.shape[1]
    piece = feat // cuts

    def columns(cut):
        return pl.ds(cut * piece, piece)

    reduce_s = [
        [
            remote(
                part.at[pl.ds((2 * section + 1) * half, half), columns(cut)],
                sib_in.at[pl.ds(section * half, half), columns(cut)],
                rs_send.at[section, cut],
                rs_recv.at[section, cut],
                sibling,
            )
            for cut in range(cuts)
        ]
        for section in range(2)
    ]
    for src in range(line):
        s_copy(0, src).wait_recv()
    up_pass(0)
    for d in range(max(line - 2, 0), line):
        at_distance(d, from_y)
    order = regroup()
    for src in range(line):
        s_copy(1, src).wait_recv()
    up_pass(2 * half)
    grouped[...] = jnp.dot(order, inner[...], preferred_element_type=f32).astype(bf16)
    loads[10].wait()
    for section in (1, 0):
        for cut in range(cuts):
            down_pass(section * 2 * half, cut)
            reduce_s[section][cut].start()

    col_source, col_owner = place(lax.broadcasted_iota(jnp.int32, (1, n * rows), 1))
    source = lax.broadcasted_iota(jnp.int32, (rows, 1), 0)
    keep = jnp.where((col_source == source) & (col_owner == me), 1.0, 0.0).astype(bf16)

    def target(k):
        return lax.rem(z + k, line)

    reduce_y = [
        [
            remote(
                pair_out.at[block(0, target(k)), columns(cut)],
                y_in.at[block(0, target(k)), columns(cut)],
                ry_send.at[k, cut],
                ry_recv.at[k, cut],
                y_peer,
            )
            for cut in range(cuts)
        ]
        for k in range(line)
    ]
    reduce_z = [
        [
            remote(
                y_out.at[block(0, target(k)), columns(cut)],
                z_in.at[block(0, k), columns(cut)],
                rz_send.at[k, cut],
                rz_recv.at[k, cut],
                target(k) * 4 + within,
            )
            for cut in range(cuts)
        ]
        for k in range(1, line)
    ]

    def to_y(k, cut):
        cols = columns(cut)
        mine, theirs = block(2, target(k)), block(1, target(k))
        pair_out[block(0, target(k)), cols] = (
            part[mine, cols].astype(f32) + sib_in[theirs, cols].astype(f32)
        ).astype(bf16)
        reduce_y[k][cut].start()

    for cut in range(cuts):
        reduce_s[1][cut].wait_recv()
        for k in range(1, line):
            to_y(k, cut)
    for cut in range(cuts):
        to_y(0, cut)
    for cut in range(cuts):
        cols = columns(cut)
        reduce_s[0][cut].wait_recv()
        for k in range(1, line):
            here = block(0, target(k))
            reduce_y[k][cut].wait_recv()
            y_out[here, cols] = (
                part[here, cols].astype(f32)
                + sib_in[here, cols].astype(f32)
                + y_in[here, cols].astype(f32)
            ).astype(bf16)
            reduce_z[k - 1][cut].start()
    residual = jnp.dot(keep, x_all[:, :feat], preferred_element_type=f32)
    for cut in range(cuts):
        reduce_y[0][cut].wait_recv()
    total = (
        residual
        + part[own, :].astype(f32)
        + sib_in[own, :].astype(f32)
        + y_in[own, :].astype(f32)
    )
    for k in range(1, line):
        for cut in range(cuts):
            reduce_z[k - 1][cut].wait_recv()
        total = total + z_in[k * rows : (k + 1) * rows, :].astype(f32)
    hidden = total.astype(bf16).astype(f32)
    scale = lax.rsqrt(jnp.mean(hidden * hidden, axis=-1, keepdims=True) + 1e-06)
    normed = (hidden * scale).astype(bf16)

    loads[11].wait()
    diagonal = lax.broadcasted_iota(jnp.int32, (rows, rows), 0) == lax.broadcasted_iota(
        jnp.int32, (rows, rows), 1
    )
    count = jnp.sum(
        jnp.where(diagonal, count_ref[...].astype(f32), 0.0), axis=1, keepdims=True
    )
    for j in range(width // tile):
        cols = slice(j * tile, (j + 1) * tile)
        talk = jnp.dot(normed, proj[:, cols], preferred_element_type=f32)
        owned = talk.astype(bf16).astype(f32)
        for f in range(horizon):
            gain = jnp.sum(taps[before - f :, cols], axis=0, keepdims=True)
            voice = base_voice[f, :, cols] + gain * owned
            voice_ref[f, :, cols] = jnp.where(count > f, voice, 0.0).astype(bf16)

    for d in range(1, line):
        to_z(d, lambda copy: copy.wait_send())
    for src in range(line):
        y_copy(src).wait_send()
        s_copy(0, src).wait_send()
        s_copy(1, src).wait_send()
    for group in reduce_s + reduce_y + reduce_z:
        for copy in group:
            copy.wait_send()


def dense_path(
    thinker_rows,
    expert_ids,
    gate_weights,
    w_gate,
    w_up,
    w_down,
    talker_proj,
    talker_slot,
    speech_count,
    left_context,
    frame_offset,
    conv_weight,
):
    n = lax.axis_size("ep")
    rows, feat = thinker_rows.shape
    hid = w_gate.shape[2]
    width = talker_proj.shape[1]
    line = n // 4
    every = n * rows
    extra = -(-3 * n // LANES) * LANES
    bf16, f32 = jnp.bfloat16, jnp.float32
    chosen = expert_ids.shape[1]
    before = left_context.shape[1]
    horizon = frame_offset.shape[0]
    cuts = 2
    vmem = pl.BlockSpec(memory_space=pltpu.VMEM)
    hbm = pl.BlockSpec(memory_space=pl.ANY)
    dma = pltpu.SemaphoreType.DMA
    voice = pl.pallas_call(
        functools.partial(dense_kernel, n),
        out_shape=jax.ShapeDtypeStruct((horizon, rows, width), bf16),
        in_specs=[hbm] * 12,
        out_specs=vmem,
        scratch_shapes=[
            pltpu.VMEM((rows, feat), bf16),
            pltpu.VMEM((chosen, rows), jnp.int32),
            pltpu.VMEM((chosen, rows), f32),
            pltpu.VMEM((1, rows), jnp.int32),
            pltpu.VMEM((1, rows), jnp.int32),
            pltpu.VMEM((before, rows, width), bf16),
            pltpu.VMEM((horizon, width), f32),
            pltpu.VMEM(conv_weight.shape, f32),
            pltpu.VMEM((horizon, rows, width), f32),
            pltpu.VMEM((feat, hid), bf16),
            pltpu.VMEM((feat, hid), bf16),
            pltpu.VMEM((hid, feat), bf16),
            pltpu.VMEM((feat, width), bf16),
            pltpu.VMEM((every, feat + extra), bf16),
            pltpu.VMEM((every, hid), bf16),
            pltpu.VMEM((every, hid), bf16),
            pltpu.VMEM((every, feat), bf16),
            pltpu.VMEM((every // 2, feat), bf16),
            pltpu.VMEM((line * rows, feat), bf16),
            pltpu.VMEM((line * rows, feat), bf16),
            pltpu.VMEM((line * rows, feat), bf16),
            pltpu.VMEM((line * rows, feat), bf16),
            dma((12,)),
            dma((line,)),
            dma((line,)),
            dma((line,)),
            dma((line,)),
            dma((2, line)),
            dma((2, line)),
            dma((2, cuts)),
            dma((2, cuts)),
            dma((line, cuts)),
            dma((line, cuts)),
            dma((line, cuts)),
            dma((line, cuts)),
        ],
        compiler_params=pltpu.CompilerParams(
            collective_id=0, has_side_effects=True, vmem_limit_bytes=60 * 1024 * 1024
        ),
    )(
        thinker_rows,
        expert_ids.T,
        gate_weights.T,
        talker_slot,
        speech_count.reshape(1, rows),
        left_context.transpose(1, 0, 2),
        frame_offset,
        conv_weight,
        w_gate,
        w_up,
        w_down,
        talker_proj,
    )
    return voice.transpose(1, 0, 2)


def local(
    thinker_rows,
    expert_ids,
    gate_weights,
    w_gate,
    w_up,
    w_down,
    talker_proj,
    talker_slot,
    speech_count,
    left_context,
    frame_offset,
    conv_weight,
):
    devices = lax.axis_size("ep")
    streams_here = thinker_rows.shape[0]
    dense = streams_here <= CAP and streams_here == devices and devices % 4 == 0
    experts = (
        thinker_rows, expert_ids, gate_weights, w_gate, w_up, w_down, talker_proj, talker_slot
    )
    voices = (speech_count, left_context, frame_offset, conv_weight)
    if dense:
        return dense_path(*experts, *voices)
    return vocode(capacity_path(*experts), *voices)


def solution(mesh):
    in_specs = (
        P(("groups", "ep"), None),
        P(("groups", "ep"), None),
        P(("groups", "ep"), None),
        P("ep", None, None),
        P("ep", None, None),
        P("ep", None, None),
        P(),
        P(("groups", "ep"), None),
        P(("groups", "ep")),
        P(("groups", "ep"), None, None),
        P(),
        P(),
    )
    out_specs = P(("groups", "ep"), None, None)
    return jax.shard_map(local, mesh=mesh, in_specs=in_specs, out_specs=out_specs, check_vma=False)
```

```python
import functools

import jax
import jax.numpy as jnp
from jax import lax
from jax.experimental import pallas as pl
from jax.experimental.pallas import tpu as pltpu
from jax.sharding import PartitionSpec as P

CAP = 16
LANES = 128


def expert_block(block_rows, gate_mat, up_mat, down_mat):
    gate_act = jnp.dot(block_rows, gate_mat, preferred_element_type=jnp.float32)
    up_act = jnp.dot(block_rows, up_mat, preferred_element_type=jnp.float32)
    inner = (jax.nn.silu(gate_act) * up_act).astype(jnp.bfloat16)
    return jnp.dot(inner, down_mat, preferred_element_type=jnp.float32).astype(jnp.bfloat16)


def project(hidden, talker_proj):
    values = hidden.astype(jnp.float32)
    scaled = values * lax.rsqrt(jnp.mean(values * values, axis=-1, keepdims=True) + 1e-06)
    return jnp.dot(
        scaled.astype(jnp.bfloat16), talker_proj, preferred_element_type=jnp.float32
    ).astype(jnp.bfloat16)


def vocode(owned, speech_count, left_context, frame_offset, conv_weight):
    frames = owned.astype(jnp.float32)[:, None, :] + frame_offset[None, :, :]
    sequence = jnp.concatenate([left_context.astype(jnp.float32), frames], axis=1)
    taps = conv_weight.shape[0]
    horizon = frame_offset.shape[0]
    result = jnp.zeros_like(frames)
    for offset in range(taps):
        result = (
            result + conv_weight[offset][None, None, :] * sequence[:, offset : offset + horizon, :]
        )
    active = jnp.arange(horizon, dtype=jnp.int32)[None, :, None] < speech_count[:, None, None]
    return jnp.where(active, result, 0.0).astype(jnp.bfloat16)


def slot_positions(expert_ids, experts):
    flat_expert = expert_ids.reshape(-1)
    onehot = (flat_expert[:, None] == jnp.arange(experts, dtype=jnp.int32)[None, :]).astype(
        jnp.int32
    )
    position = jnp.sum((jnp.cumsum(onehot, axis=0) - onehot) * onehot, axis=1)
    return (flat_expert, position)


def run_and_return(buffer, w_gate, w_up, w_down):
    sources, slot_count, features = buffer.shape
    flattened = buffer.reshape(sources * slot_count, features)
    outputs = expert_block(flattened, w_gate[0], w_up[0], w_down[0]).reshape(
        sources, slot_count, features
    )
    return lax.all_to_all(outputs, "ep", split_axis=0, concat_axis=0, tiled=True)


def capacity_path(
    thinker_rows, expert_ids, gate_weights, w_gate, w_up, w_down, talker_proj, talker_slot
):
    devices = lax.axis_size("ep")
    streams_here, features = thinker_rows.shape
    chosen = expert_ids.shape[1]
    flat_expert, position = slot_positions(expert_ids, devices)
    row_index = jnp.arange(streams_here * chosen, dtype=jnp.int32) // chosen
    outgoing = (
        jnp.zeros((devices, CAP, features), jnp.bfloat16)
        .at[flat_expert, position]
        .set(thinker_rows[row_index])
    )
    returned = run_and_return(
        lax.all_to_all(outgoing, "ep", split_axis=0, concat_axis=0, tiled=True),
        w_gate,
        w_up,
        w_down,
    )
    lookup = (
        returned[flat_expert, position].astype(jnp.float32).reshape(streams_here, chosen, features)
    )
    mixture = jnp.sum(gate_weights[:, :, None] * lookup, axis=1)
    hidden = (thinker_rows.astype(jnp.float32) + mixture).astype(jnp.bfloat16)
    slots = talker_slot[0]
    per_owner = streams_here // devices
    talker_rows = project(hidden, talker_proj)
    placed = (
        jnp.zeros_like(talker_rows)
        .at[slots]
        .set(talker_rows)
        .reshape(devices, per_owner, talker_rows.shape[1])
    )
    return lax.all_to_all(placed, "ep", split_axis=0, concat_axis=0, tiled=True).reshape(
        streams_here, talker_rows.shape[1]
    )


def dense_kernel(
    n,
    rows_hbm,
    ids_hbm,
    gates_hbm,
    slot_hbm,
    count_hbm,
    context_hbm,
    offset_hbm,
    taps_hbm,
    wg_hbm,
    wu_hbm,
    wd_hbm,
    proj_hbm,
    voice_ref,
    rows_ref,
    ids_ref,
    gates_ref,
    slot_ref,
    count_ref,
    context,
    frame_offset,
    taps,
    base_voice,
    voices,
    wg,
    wu,
    wd,
    proj,
    x_all,
    inner,
    grouped,
    part,
    sib_in,
    pair_out,
    y_in,
    y_out,
    z_in,
    load_sem,
    gz_send,
    gz_recv,
    gy_send,
    gy_recv,
    gs_send,
    gs_recv,
    rs_send,
    rs_recv,
    ry_send,
    ry_recv,
    rz_send,
    rz_recv,
):
    f32, bf16 = jnp.float32, jnp.bfloat16
    rows, feat = rows_hbm.shape
    hid = wg.shape[1]
    width = proj.shape[1]
    line = n // 4
    half = line * rows
    tile = min(256, hid)
    me = lax.axis_index("ep")
    z = me // 4
    within = me % 4
    y = within // 2
    core = within % 2
    y_peer = me + 2 - 4 * y
    sibling = me + 1 - 2 * core

    def block(section, pos):
        return pl.ds(pl.multiple_of(section * half + pos * rows, rows), rows)

    own = block(0, z)
    loads = [
        pltpu.make_async_copy(src, dst, load_sem.at[i])
        for i, (src, dst) in enumerate(
            (
                (rows_hbm, rows_ref),
                (ids_hbm, ids_ref),
                (gates_hbm, gates_ref),
                (slot_hbm, slot_ref),
                (count_hbm, count_ref),
                (context_hbm, context),
                (offset_hbm, frame_offset),
                (taps_hbm, taps),
                (wg_hbm.at[0], wg),
                (wu_hbm.at[0], wu),
                (wd_hbm.at[0], wd),
                (proj_hbm, proj),
            )
        )
    ]
    for load in loads[:4]:
        load.start()

    z_peers = [lax.rem(z + k, line) * 4 + within for k in range(1, line)]
    partners = z_peers + [y_peer, sibling]
    barrier = pltpu.get_barrier_semaphore()
    for peer in partners:
        pl.semaphore_signal(barrier, inc=1, device_id={"ep": peer})

    extra = x_all.shape[1] - feat
    spot = lax.broadcasted_iota(jnp.int32, (extra, rows), 0)
    expert_of = lax.rem(spot, n)
    weight = jnp.zeros((extra, rows), f32)
    for load in loads[:4]:
        load.wait()
    for j in range(ids_ref.shape[0]):
        weight = weight + jnp.where(
            ids_ref[j : j + 1, :] == expert_of, gates_ref[j : j + 1, :], 0.0
        )
    high = weight.astype(bf16).astype(f32)
    mid = (weight - high).astype(bf16).astype(f32)
    low = weight - high - mid
    coded = jnp.where(spot < n, high, jnp.where(spot < 2 * n, mid, jnp.where(spot < 3 * n, low, 0.0)))
    owner = lax.broadcasted_iota(jnp.int32, (n, rows), 0)
    pick = jnp.where(owner == slot_ref[...], 1.0, 0.0).astype(bf16)
    x_all[own, :feat] = jnp.dot(pick, rows_ref[...], preferred_element_type=f32).astype(bf16)
    x_all[own, feat:] = lax.dot_general(
        pick, coded.astype(bf16), (((1,), (1,)), ((), ())), preferred_element_type=f32
    ).astype(bf16)

    pl.semaphore_wait(barrier, len(partners))

    def remote(src, dst, send, recv, peer):
        return pltpu.make_async_remote_copy(
            src_ref=src, dst_ref=dst, send_sem=send, recv_sem=recv, device_id={"ep": peer}
        )

    def z_copy(peer, src):
        here = x_all.at[block(0, src)]
        return remote(here, here, gz_send.at[peer], gz_recv.at[src], peer * 4 + within)

    def y_copy(src):
        return remote(
            x_all.at[block(0, src)],
            x_all.at[block(2, src)],
            gy_send.at[src],
            gy_recv.at[src],
            y_peer,
        )

    def s_copy(section, src):
        return remote(
            x_all.at[block(2 * section, src)],
            x_all.at[block(2 * section + 1, src)],
            gs_send.at[section, src],
            gs_recv.at[section, src],
            sibling,
        )

    def at_distance(d, use):
        for src in (z,) if d == 0 else (z - d, z + d):
            pl.when((src >= 0) & (src < line))(functools.partial(use, src))

    def to_z(d, act):
        at_distance(d, lambda peer: act(z_copy(peer, z)))

    def from_z(d):
        at_distance(d, lambda src: z_copy(src, src).wait_recv())

    def hand_on(src):
        y_copy(src).start()
        s_copy(0, src).start()

    def from_y(src):
        y_copy(src).wait_recv()
        s_copy(1, src).start()

    to_z(1, lambda copy: copy.start())
    hand_on(z)
    for d in range(2, line):
        to_z(d, lambda copy: copy.start())
    for load in loads[4:]:
        load.start()

    for load in loads[4:8]:
        load.wait()
    before = context.shape[0]
    horizon = frame_offset.shape[0]
    for f in range(horizon):
        voice = jnp.zeros((rows, width), f32)
        for t in range(taps.shape[0]):
            tap = taps[t : t + 1, :]
            if f + t < before:
                voice = voice + tap * context[f + t].astype(f32)
            else:
                voice = voice + tap * frame_offset[f + t - before : f + t - before + 1, :]
        base_voice[f] = voice

    for d in range(1, line):
        from_z(d)
        at_distance(d, hand_on)
        if d < line - 1:
            at_distance(d - 1, from_y)

    loads[8].wait()
    loads[9].wait()

    def up_pass(base):
        span = pl.ds(base, 2 * half)
        lanes = lax.broadcasted_iota(jnp.int32, (2 * half, extra), 1)
        mine = (lax.rem(lanes, n) == me) & (lanes < 3 * n)
        coef = jnp.sum(
            jnp.where(mine, x_all[span, feat:].astype(f32), 0.0), axis=1, keepdims=True
        )

        def step(j, carry):
            cols = pl.ds(pl.multiple_of(j * tile, tile), tile)
            x = x_all[span, :feat]
            gate_act = jnp.dot(x, wg[:, cols], preferred_element_type=f32)
            up_act = jnp.dot(x, wu[:, cols], preferred_element_type=f32)
            inner[span, cols] = (jax.nn.silu(gate_act) * up_act * coef).astype(bf16)
            return carry

        lax.fori_loop(0, hid // tile, step, 0)

    def place(index):
        section = index // half
        device = (
            (index % half) // rows * 4
            + jnp.where(section // 2 == 0, y, 1 - y) * 2
            + jnp.where(section % 2 == 0, core, 1 - core)
        )
        return device, index % rows

    def regroup():
        every = n * rows
        row_owner, row_source = place(lax.broadcasted_iota(jnp.int32, (every, 1), 0))
        col_source, col_owner = place(lax.broadcasted_iota(jnp.int32, (1, every), 1))
        match = (row_owner == col_owner) & (row_source == col_source)
        return jnp.where(match, 1.0, 0.0).astype(bf16)

    def down_pass(base, cut):
        span = pl.ds(base, 2 * half)

        def step(j, carry):
            cols = pl.ds(pl.multiple_of(cut * piece + j * tile, tile), tile)
            out = jnp.dot(grouped[span, :], wd[:, cols], preferred_element_type=f32)
            part[span, cols] = out.astype(bf16)
            return carry

        lax.fori_loop(0, piece // tile, step, 0)

    cuts = rs_send.shape[1]
    piece = feat // cuts

    def columns(cut):
        return pl.ds(cut * piece, piece)

    reduce_s = [
        [
            remote(
                part.at[pl.ds((2 * section + 1) * half, half), columns(cut)],
                sib_in.at[pl.ds(section * half, half), columns(cut)],
                rs_send.at[section, cut],
                rs_recv.at[section, cut],
                sibling,
            )
            for cut in range(cuts)
        ]
        for section in range(2)
    ]
    for src in range(line):
        s_copy(0, src).wait_recv()
    up_pass(0)
    for d in range(max(line - 2, 0), line):
        at_distance(d, from_y)
    order = regroup()
    for src in range(line):
        s_copy(1, src).wait_recv()
    up_pass(2 * half)
    grouped[...] = jnp.dot(order, inner[...], preferred_element_type=f32).astype(bf16)
    loads[10].wait()
    for cut in range(cuts):
        down_pass(2 * half, cut)
        reduce_s[1][cut].start()

    col_source, col_owner = place(lax.broadcasted_iota(jnp.int32, (1, n * rows), 1))
    source = lax.broadcasted_iota(jnp.int32, (rows, 1), 0)
    keep = jnp.where((col_source == source) & (col_owner == me), 1.0, 0.0).astype(bf16)

    def target(k):
        return lax.rem(z + k, line)

    reduce_y = [
        [
            remote(
                pair_out.at[block(0, target(k)), columns(cut)],
                y_in.at[block(0, target(k)), columns(cut)],
                ry_send.at[k, cut],
                ry_recv.at[k, cut],
                y_peer,
            )
            for cut in range(cuts)
        ]
        for k in range(line)
    ]
    reduce_z = [
        [
            remote(
                y_out.at[block(0, target(k)), columns(cut)],
                z_in.at[block(0, k), columns(cut)],
                rz_send.at[k, cut],
                rz_recv.at[k, cut],
                target(k) * 4 + within,
            )
            for cut in range(cuts)
        ]
        for k in range(1, line)
    ]

    def to_y(k, cut):
        cols = columns(cut)
        mine, theirs = block(2, target(k)), block(1, target(k))
        pair_out[block(0, target(k)), cols] = (
            part[mine, cols].astype(f32) + sib_in[theirs, cols].astype(f32)
        ).astype(bf16)
        reduce_y[k][cut].start()

    for cut in range(cuts):
        down_pass(0, cut)
        reduce_s[0][cut].start()
        reduce_s[1][cut].wait_recv()
        for k in range(1, line):
            to_y(k, cut)
    for cut in range(cuts):
        to_y(0, cut)
    for cut in range(cuts):
        cols = columns(cut)
        reduce_s[0][cut].wait_recv()
        for k in range(1, line):
            here = block(0, target(k))
            reduce_y[k][cut].wait_recv()
            y_out[here, cols] = (
                part[here, cols].astype(f32)
                + sib_in[here, cols].astype(f32)
                + y_in[here, cols].astype(f32)
            ).astype(bf16)
            reduce_z[k - 1][cut].start()
    residual = jnp.dot(keep, x_all[:, :feat], preferred_element_type=f32)
    for cut in range(cuts):
        reduce_y[0][cut].wait_recv()
    total = (
        residual
        + part[own, :].astype(f32)
        + sib_in[own, :].astype(f32)
        + y_in[own, :].astype(f32)
    )
    for k in range(1, line):
        for cut in range(cuts):
            reduce_z[k - 1][cut].wait_recv()
        total = total + z_in[k * rows : (k + 1) * rows, :].astype(f32)
    hidden = total.astype(bf16).astype(f32)
    scale = lax.rsqrt(jnp.mean(hidden * hidden, axis=-1, keepdims=True) + 1e-06)
    normed = (hidden * scale).astype(bf16)

    loads[11].wait()
    diagonal = lax.broadcasted_iota(jnp.int32, (rows, rows), 0) == lax.broadcasted_iota(
        jnp.int32, (rows, rows), 1
    )
    count = jnp.sum(
        jnp.where(diagonal, count_ref[...].astype(f32), 0.0), axis=1, keepdims=True
    )
    for j in range(width // tile):
        cols = slice(j * tile, (j + 1) * tile)
        talk = jnp.dot(normed, proj[:, cols], preferred_element_type=f32)
        owned = talk.astype(bf16).astype(f32)
        for f in range(horizon):
            gain = jnp.sum(taps[before - f :, cols], axis=0, keepdims=True)
            voice = base_voice[f, :, cols] + gain * owned
            voices[:, f, cols] = jnp.where(count > f, voice, 0.0)
        voice_ref[:, :, cols] = voices[:, :, cols].astype(bf16)

    for d in range(1, line):
        to_z(d, lambda copy: copy.wait_send())
    for src in range(line):
        y_copy(src).wait_send()
        s_copy(0, src).wait_send()
        s_copy(1, src).wait_send()
    for group in reduce_s + reduce_y + reduce_z:
        for copy in group:
            copy.wait_send()


def dense_path(
    thinker_rows,
    expert_ids,
    gate_weights,
    w_gate,
    w_up,
    w_down,
    talker_proj,
    talker_slot,
    speech_count,
    left_context,
    frame_offset,
    conv_weight,
):
    n = lax.axis_size("ep")
    rows, feat = thinker_rows.shape
    hid = w_gate.shape[2]
    width = talker_proj.shape[1]
    line = n // 4
    every = n * rows
    extra = -(-3 * n // LANES) * LANES
    bf16, f32 = jnp.bfloat16, jnp.float32
    chosen = expert_ids.shape[1]
    before = left_context.shape[1]
    horizon = frame_offset.shape[0]
    cuts = 2
    vmem = pl.BlockSpec(memory_space=pltpu.VMEM)
    hbm = pl.BlockSpec(memory_space=pl.ANY)
    dma = pltpu.SemaphoreType.DMA
    return pl.pallas_call(
        functools.partial(dense_kernel, n),
        out_shape=jax.ShapeDtypeStruct((rows, horizon, width), bf16),
        in_specs=[hbm] * 12,
        out_specs=vmem,
        scratch_shapes=[
            pltpu.VMEM((rows, feat), bf16),
            pltpu.VMEM((chosen, rows), jnp.int32),
            pltpu.VMEM((chosen, rows), f32),
            pltpu.VMEM((1, rows), jnp.int32),
            pltpu.VMEM((1, rows), jnp.int32),
            pltpu.VMEM((before, rows, width), bf16),
            pltpu.VMEM((horizon, width), f32),
            pltpu.VMEM(conv_weight.shape, f32),
            pltpu.VMEM((horizon, rows, width), f32),
            pltpu.VMEM((rows, horizon, width), f32),
            pltpu.VMEM((feat, hid), bf16),
            pltpu.VMEM((feat, hid), bf16),
            pltpu.VMEM((hid, feat), bf16),
            pltpu.VMEM((feat, width), bf16),
            pltpu.VMEM((every, feat + extra), bf16),
            pltpu.VMEM((every, hid), bf16),
            pltpu.VMEM((every, hid), bf16),
            pltpu.VMEM((every, feat), bf16),
            pltpu.VMEM((every // 2, feat), bf16),
            pltpu.VMEM((line * rows, feat), bf16),
            pltpu.VMEM((line * rows, feat), bf16),
            pltpu.VMEM((line * rows, feat), bf16),
            pltpu.VMEM((line * rows, feat), bf16),
            dma((12,)),
            dma((line,)),
            dma((line,)),
            dma((line,)),
            dma((line,)),
            dma((2, line)),
            dma((2, line)),
            dma((2, cuts)),
            dma((2, cuts)),
            dma((line, cuts)),
            dma((line, cuts)),
            dma((line, cuts)),
            dma((line, cuts)),
        ],
        compiler_params=pltpu.CompilerParams(
            collective_id=0, has_side_effects=True, vmem_limit_bytes=60 * 1024 * 1024
        ),
    )(
        thinker_rows,
        expert_ids.T,
        gate_weights.T,
        talker_slot,
        speech_count.reshape(1, rows),
        left_context.transpose(1, 0, 2),
        frame_offset,
        conv_weight,
        w_gate,
        w_up,
        w_down,
        talker_proj,
    )


def local(
    thinker_rows,
    expert_ids,
    gate_weights,
    w_gate,
    w_up,
    w_down,
    talker_proj,
    talker_slot,
    speech_count,
    left_context,
    frame_offset,
    conv_weight,
):
    devices = lax.axis_size("ep")
    streams_here = thinker_rows.shape[0]
    dense = streams_here <= CAP and streams_here == devices and devices % 4 == 0
    experts = (
        thinker_rows, expert_ids, gate_weights, w_gate, w_up, w_down, talker_proj, talker_slot
    )
    voices = (speech_count, left_context, frame_offset, conv_weight)
    if dense:
        return dense_path(*experts, *voices)
    return vocode(capacity_path(*experts), *voices)


def solution(mesh):
    in_specs = (
        P(("groups", "ep"), None),
        P(("groups", "ep"), None),
        P(("groups", "ep"), None),
        P("ep", None, None),
        P("ep", None, None),
        P("ep", None, None),
        P(),
        P(("groups", "ep"), None),
        P(("groups", "ep")),
        P(("groups", "ep"), None, None),
        P(),
        P(),
    )
    out_specs = P(("groups", "ep"), None, None)
    return jax.shard_map(local, mesh=mesh, in_specs=in_specs, out_specs=out_specs, check_vma=False)
```

```python
import functools

import jax
import jax.numpy as jnp
from jax import lax
from jax.experimental import pallas as pl
from jax.experimental.pallas import tpu as pltpu
from jax.sharding import PartitionSpec as P

CAP = 16
LANES = 128


def expert_block(block_rows, gate_mat, up_mat, down_mat):
    gate_act = jnp.dot(block_rows, gate_mat, preferred_element_type=jnp.float32)
    up_act = jnp.dot(block_rows, up_mat, preferred_element_type=jnp.float32)
    inner = (jax.nn.silu(gate_act) * up_act).astype(jnp.bfloat16)
    return jnp.dot(inner, down_mat, preferred_element_type=jnp.float32).astype(jnp.bfloat16)


def project(hidden, talker_proj):
    values = hidden.astype(jnp.float32)
    scaled = values * lax.rsqrt(jnp.mean(values * values, axis=-1, keepdims=True) + 1e-06)
    return jnp.dot(
        scaled.astype(jnp.bfloat16), talker_proj, preferred_element_type=jnp.float32
    ).astype(jnp.bfloat16)


def vocode(owned, speech_count, left_context, frame_offset, conv_weight):
    frames = owned.astype(jnp.float32)[:, None, :] + frame_offset[None, :, :]
    sequence = jnp.concatenate([left_context.astype(jnp.float32), frames], axis=1)
    taps = conv_weight.shape[0]
    horizon = frame_offset.shape[0]
    result = jnp.zeros_like(frames)
    for offset in range(taps):
        result = (
            result + conv_weight[offset][None, None, :] * sequence[:, offset : offset + horizon, :]
        )
    active = jnp.arange(horizon, dtype=jnp.int32)[None, :, None] < speech_count[:, None, None]
    return jnp.where(active, result, 0.0).astype(jnp.bfloat16)


def slot_positions(expert_ids, experts):
    flat_expert = expert_ids.reshape(-1)
    onehot = (flat_expert[:, None] == jnp.arange(experts, dtype=jnp.int32)[None, :]).astype(
        jnp.int32
    )
    position = jnp.sum((jnp.cumsum(onehot, axis=0) - onehot) * onehot, axis=1)
    return (flat_expert, position)


def run_and_return(buffer, w_gate, w_up, w_down):
    sources, slot_count, features = buffer.shape
    flattened = buffer.reshape(sources * slot_count, features)
    outputs = expert_block(flattened, w_gate[0], w_up[0], w_down[0]).reshape(
        sources, slot_count, features
    )
    return lax.all_to_all(outputs, "ep", split_axis=0, concat_axis=0, tiled=True)


def capacity_path(
    thinker_rows, expert_ids, gate_weights, w_gate, w_up, w_down, talker_proj, talker_slot
):
    devices = lax.axis_size("ep")
    streams_here, features = thinker_rows.shape
    chosen = expert_ids.shape[1]
    flat_expert, position = slot_positions(expert_ids, devices)
    row_index = jnp.arange(streams_here * chosen, dtype=jnp.int32) // chosen
    outgoing = (
        jnp.zeros((devices, CAP, features), jnp.bfloat16)
        .at[flat_expert, position]
        .set(thinker_rows[row_index])
    )
    returned = run_and_return(
        lax.all_to_all(outgoing, "ep", split_axis=0, concat_axis=0, tiled=True),
        w_gate,
        w_up,
        w_down,
    )
    lookup = (
        returned[flat_expert, position].astype(jnp.float32).reshape(streams_here, chosen, features)
    )
    mixture = jnp.sum(gate_weights[:, :, None] * lookup, axis=1)
    hidden = (thinker_rows.astype(jnp.float32) + mixture).astype(jnp.bfloat16)
    slots = talker_slot[0]
    per_owner = streams_here // devices
    talker_rows = project(hidden, talker_proj)
    placed = (
        jnp.zeros_like(talker_rows)
        .at[slots]
        .set(talker_rows)
        .reshape(devices, per_owner, talker_rows.shape[1])
    )
    return lax.all_to_all(placed, "ep", split_axis=0, concat_axis=0, tiled=True).reshape(
        streams_here, talker_rows.shape[1]
    )


def dense_kernel(
    n,
    rows_hbm,
    ids_hbm,
    gates_hbm,
    slot_hbm,
    count_hbm,
    context_hbm,
    offset_hbm,
    taps_hbm,
    wg_hbm,
    wu_hbm,
    wd_hbm,
    proj_hbm,
    voice_ref,
    rows_ref,
    ids_ref,
    gates_ref,
    slot_ref,
    count_ref,
    context,
    frame_offset,
    taps,
    base_voice,
    voices,
    wg,
    wu,
    wd,
    proj,
    x_all,
    inner,
    grouped,
    part,
    sib_in,
    pair_out,
    y_in,
    y_out,
    z_in,
    relay_in,
    load_sem,
    gz_send,
    gz_recv,
    gy_send,
    gy_recv,
    gs_send,
    gs_recv,
    rs_send,
    rs_recv,
    ry_send,
    ry_recv,
    rz_send,
    rz_recv,
    relay_recv,
):
    f32, bf16 = jnp.float32, jnp.bfloat16
    rows, feat = rows_hbm.shape
    hid = wg.shape[1]
    width = proj.shape[1]
    line = n // 4
    half = line * rows
    tile = min(256, hid)
    me = lax.axis_index("ep")
    z = me // 4
    within = me % 4
    y = within // 2
    core = within % 2
    y_peer = me + 2 - 4 * y
    sibling = me + 1 - 2 * core

    def block(section, pos):
        return pl.ds(pl.multiple_of(section * half + pos * rows, rows), rows)

    own = block(0, z)
    loads = [
        pltpu.make_async_copy(src, dst, load_sem.at[i])
        for i, (src, dst) in enumerate(
            (
                (rows_hbm, rows_ref),
                (ids_hbm, ids_ref),
                (gates_hbm, gates_ref),
                (slot_hbm, slot_ref),
                (count_hbm, count_ref),
                (context_hbm, context),
                (offset_hbm, frame_offset),
                (taps_hbm, taps),
                (wg_hbm.at[0], wg),
                (wu_hbm.at[0], wu),
                (wd_hbm.at[0], wd),
                (proj_hbm, proj),
            )
        )
    ]
    for load in loads[:4]:
        load.start()

    @pl.when((z == 0) | (z == line - 1))
    def _():
        relay_in[...] = jnp.zeros_like(relay_in)
        z_in[block(0, line - 1 - z), :] = jnp.zeros((rows, feat), bf16)

    z_peers = [lax.rem(z + k, line) * 4 + within for k in range(1, line)]
    partners = z_peers + [y_peer, sibling]
    barrier = pltpu.get_barrier_semaphore()
    for peer in partners:
        pl.semaphore_signal(barrier, inc=1, device_id={"ep": peer})

    extra = x_all.shape[1] - feat
    spot = lax.broadcasted_iota(jnp.int32, (extra, rows), 0)
    expert_of = lax.rem(spot, n)
    weight = jnp.zeros((extra, rows), f32)
    for load in loads[:4]:
        load.wait()
    for j in range(ids_ref.shape[0]):
        weight = weight + jnp.where(
            ids_ref[j : j + 1, :] == expert_of, gates_ref[j : j + 1, :], 0.0
        )
    high = weight.astype(bf16).astype(f32)
    mid = (weight - high).astype(bf16).astype(f32)
    low = weight - high - mid
    coded = jnp.where(spot < n, high, jnp.where(spot < 2 * n, mid, jnp.where(spot < 3 * n, low, 0.0)))
    owner = lax.broadcasted_iota(jnp.int32, (n, rows), 0)
    pick = jnp.where(owner == slot_ref[...], 1.0, 0.0).astype(bf16)
    x_all[own, :feat] = jnp.dot(pick, rows_ref[...], preferred_element_type=f32).astype(bf16)
    x_all[own, feat:] = lax.dot_general(
        pick, coded.astype(bf16), (((1,), (1,)), ((), ())), preferred_element_type=f32
    ).astype(bf16)

    pl.semaphore_wait(barrier, len(partners))

    def remote(src, dst, send, recv, peer):
        return pltpu.make_async_remote_copy(
            src_ref=src, dst_ref=dst, send_sem=send, recv_sem=recv, device_id={"ep": peer}
        )

    def z_copy(peer, src):
        here = x_all.at[block(0, src)]
        slot = peer if src is z else line
        return remote(here, here, gz_send.at[slot], gz_recv.at[src], peer * 4 + within)

    def y_copy(src):
        return remote(
            x_all.at[block(0, src)],
            x_all.at[block(2, src)],
            gy_send.at[src],
            gy_recv.at[src],
            y_peer,
        )

    def s_copy(section, src):
        return remote(
            x_all.at[block(2 * section, src)],
            x_all.at[block(2 * section + 1, src)],
            gs_send.at[section, src],
            gs_recv.at[section, src],
            sibling,
        )

    def at_distance(d, use):
        for src in (z,) if d == 0 else (z - d, z + d):
            pl.when((src >= 0) & (src < line))(functools.partial(use, src))

    def to_z(d, act):
        at_distance(d, lambda peer: act(z_copy(peer, z)))

    def from_z(d):
        at_distance(d, lambda src: z_copy(src, src).wait_recv())

    def relay_z(act):
        pl.when(z == line - 2)(lambda: act(z_copy(z + 1, 0)))
        pl.when(z == 1)(lambda: act(z_copy(z - 1, line - 1)))

    def hand_on(src):
        y_copy(src).start()
        s_copy(0, src).start()

    def from_y(src):
        y_copy(src).wait_recv()
        s_copy(1, src).start()

    to_z(1, lambda copy: copy.start())
    hand_on(z)
    for d in range(2, line - 1):
        to_z(d, lambda copy: copy.start())
    for load in loads[4:]:
        load.start()

    for load in loads[4:8]:
        load.wait()
    before = context.shape[0]
    horizon = frame_offset.shape[0]
    for f in range(horizon):
        voice = jnp.zeros((rows, width), f32)
        for t in range(taps.shape[0]):
            tap = taps[t : t + 1, :]
            if f + t < before:
                voice = voice + tap * context[f + t].astype(f32)
            else:
                voice = voice + tap * frame_offset[f + t - before : f + t - before + 1, :]
        base_voice[f] = voice

    for d in range(1, line):
        from_z(d)
        if d == line - 2:
            relay_z(lambda copy: copy.start())
        at_distance(d, hand_on)
        if d < line - 1:
            at_distance(d - 1, from_y)

    loads[8].wait()
    loads[9].wait()

    def up_pass(base):
        span = pl.ds(base, 2 * half)
        lanes = lax.broadcasted_iota(jnp.int32, (2 * half, extra), 1)
        mine = (lax.rem(lanes, n) == me) & (lanes < 3 * n)
        coef = jnp.sum(
            jnp.where(mine, x_all[span, feat:].astype(f32), 0.0), axis=1, keepdims=True
        )

        def step(j, carry):
            cols = pl.ds(pl.multiple_of(j * tile, tile), tile)
            x = x_all[span, :feat]
            gate_act = jnp.dot(x, wg[:, cols], preferred_element_type=f32)
            up_act = jnp.dot(x, wu[:, cols], preferred_element_type=f32)
            inner[span, cols] = (jax.nn.silu(gate_act) * up_act * coef).astype(bf16)
            return carry

        lax.fori_loop(0, hid // tile, step, 0)

    def place(index):
        section = index // half
        device = (
            (index % half) // rows * 4
            + jnp.where(section // 2 == 0, y, 1 - y) * 2
            + jnp.where(section % 2 == 0, core, 1 - core)
        )
        return device, index % rows

    def regroup():
        every = n * rows
        row_owner, row_source = place(lax.broadcasted_iota(jnp.int32, (every, 1), 0))
        col_source, col_owner = place(lax.broadcasted_iota(jnp.int32, (1, every), 1))
        match = (row_owner == col_owner) & (row_source == col_source)
        return jnp.where(match, 1.0, 0.0).astype(bf16)

    def down_pass(base, cut):
        span = pl.ds(base, 2 * half)

        def step(j, carry):
            cols = pl.ds(pl.multiple_of(cut * piece + j * tile, tile), tile)
            out = jnp.dot(grouped[span, :], wd[:, cols], preferred_element_type=f32)
            part[span, cols] = out.astype(bf16)
            return carry

        lax.fori_loop(0, piece // tile, step, 0)

    cuts = rs_send.shape[1]
    piece = feat // cuts

    def columns(cut):
        return pl.ds(cut * piece, piece)

    reduce_s = [
        [
            remote(
                part.at[pl.ds((2 * section + 1) * half, half), columns(cut)],
                sib_in.at[pl.ds(section * half, half), columns(cut)],
                rs_send.at[section, cut],
                rs_recv.at[section, cut],
                sibling,
            )
            for cut in range(cuts)
        ]
        for section in range(2)
    ]
    for src in range(line):
        s_copy(0, src).wait_recv()
    up_pass(0)
    for d in range(max(line - 2, 0), line):
        at_distance(d, from_y)
    order = regroup()
    for src in range(line):
        s_copy(1, src).wait_recv()
    up_pass(2 * half)
    grouped[...] = jnp.dot(order, inner[...], preferred_element_type=f32).astype(bf16)
    loads[10].wait()
    for cut in range(cuts):
        down_pass(2 * half, cut)
        reduce_s[1][cut].start()

    col_source, col_owner = place(lax.broadcasted_iota(jnp.int32, (1, n * rows), 1))
    source = lax.broadcasted_iota(jnp.int32, (rows, 1), 0)
    keep = jnp.where((col_source == source) & (col_owner == me), 1.0, 0.0).astype(bf16)

    last = line - 1
    upper = z // 2
    inside = z * (last - z) // 2

    def target(k):
        if k == 0:
            return z
        low = {1: last - last * inside, 2: 2, 3: 1 + 2 * inside}[k]
        return upper * (last - low) + (1 - upper) * low

    reduce_y = [
        [
            remote(
                pair_out.at[block(0, target(k)), columns(cut)],
                y_in.at[block(0, target(k)), columns(cut)],
                ry_send.at[k, cut],
                ry_recv.at[k, cut],
                y_peer,
            )
            for cut in range(cuts)
        ]
        for k in range(line)
    ]
    reduce_z = [
        [
            remote(
                y_out.at[block(0, target(k)), columns(cut)],
                z_in.at[own, columns(cut)],
                rz_send.at[k, cut],
                rz_recv.at[z, cut],
                target(k) * 4 + within,
            )
            for cut in range(cuts)
        ]
        for k in range(1, line)
    ]

    def relay(cut):
        return remote(
            y_out.at[block(0, target(1)), columns(cut)],
            relay_in.at[:, columns(cut)],
            rz_send.at[1, cut],
            relay_recv.at[cut],
            (1 + upper) * 4 + within,
        )

    def arrived_z(src, cut):
        here = z_in.at[block(0, src), columns(cut)]
        remote(here, here, rz_send.at[0, cut], rz_recv.at[src, cut], sibling).wait_recv()

    def to_y(k, cut):
        cols = columns(cut)
        mine, theirs = block(2, target(k)), block(1, target(k))
        pair_out[block(0, target(k)), cols] = (
            part[mine, cols].astype(f32) + sib_in[theirs, cols].astype(f32)
        ).astype(bf16)
        reduce_y[k][cut].start()

    for cut in range(cuts):
        down_pass(0, cut)
        reduce_s[0][cut].start()
        reduce_s[1][cut].wait_recv()
        for k in range(1, line):
            to_y(k, cut)
    for cut in range(cuts):
        to_y(0, cut)
    for cut in range(cuts):
        cols = columns(cut)
        reduce_s[0][cut].wait_recv()
        for k in range(1, line):
            here = block(0, target(k))
            reduce_y[k][cut].wait_recv()
            partial = (
                part[here, cols].astype(f32)
                + sib_in[here, cols].astype(f32)
                + y_in[here, cols].astype(f32)
            )
            if k == last:
                pl.when(inside == 1)(lambda cut=cut: relay(cut).wait_recv())
                partial = partial + relay_in[:, cols].astype(f32)
            y_out[here, cols] = partial.astype(bf16)
            if k == 1:
                pl.when(inside == 0)(lambda cut=cut: relay(cut).start())
                pl.when(inside == 1)(lambda cut=cut: reduce_z[0][cut].start())
            else:
                reduce_z[k - 1][cut].start()
    residual = jnp.dot(keep, x_all[:, :feat], preferred_element_type=f32)
    for cut in range(cuts):
        reduce_y[0][cut].wait_recv()
    total = (
        residual
        + part[own, :].astype(f32)
        + sib_in[own, :].astype(f32)
        + y_in[own, :].astype(f32)
    )
    for k in range(1, line):
        src = lax.rem(z + k, line)
        for cut in range(cuts):
            direct = (inside == 1) | (src + z != last)
            pl.when(direct)(functools.partial(arrived_z, src, cut))
        total = total + z_in[block(0, src), :].astype(f32)
    hidden = total.astype(bf16).astype(f32)
    scale = lax.rsqrt(jnp.mean(hidden * hidden, axis=-1, keepdims=True) + 1e-06)
    normed = (hidden * scale).astype(bf16)

    loads[11].wait()
    diagonal = lax.broadcasted_iota(jnp.int32, (rows, rows), 0) == lax.broadcasted_iota(
        jnp.int32, (rows, rows), 1
    )
    count = jnp.sum(
        jnp.where(diagonal, count_ref[...].astype(f32), 0.0), axis=1, keepdims=True
    )
    for j in range(width // tile):
        cols = slice(j * tile, (j + 1) * tile)
        talk = jnp.dot(normed, proj[:, cols], preferred_element_type=f32)
        owned = talk.astype(bf16).astype(f32)
        for f in range(horizon):
            gain = jnp.sum(taps[before - f :, cols], axis=0, keepdims=True)
            voice = base_voice[f, :, cols] + gain * owned
            voices[:, f, cols] = jnp.where(count > f, voice, 0.0)
        voice_ref[:, :, cols] = voices[:, :, cols].astype(bf16)

    for d in range(1, line - 1):
        to_z(d, lambda copy: copy.wait_send())
    relay_z(lambda copy: copy.wait_send())
    for src in range(line):
        y_copy(src).wait_send()
        s_copy(0, src).wait_send()
        s_copy(1, src).wait_send()
    for group in reduce_s + reduce_y + reduce_z:
        for copy in group:
            copy.wait_send()


def dense_path(
    thinker_rows,
    expert_ids,
    gate_weights,
    w_gate,
    w_up,
    w_down,
    talker_proj,
    talker_slot,
    speech_count,
    left_context,
    frame_offset,
    conv_weight,
):
    n = lax.axis_size("ep")
    rows, feat = thinker_rows.shape
    hid = w_gate.shape[2]
    width = talker_proj.shape[1]
    line = n // 4
    every = n * rows
    extra = -(-3 * n // LANES) * LANES
    bf16, f32 = jnp.bfloat16, jnp.float32
    chosen = expert_ids.shape[1]
    before = left_context.shape[1]
    horizon = frame_offset.shape[0]
    cuts = 2
    vmem = pl.BlockSpec(memory_space=pltpu.VMEM)
    hbm = pl.BlockSpec(memory_space=pl.ANY)
    dma = pltpu.SemaphoreType.DMA
    return pl.pallas_call(
        functools.partial(dense_kernel, n),
        out_shape=jax.ShapeDtypeStruct((rows, horizon, width), bf16),
        in_specs=[hbm] * 12,
        out_specs=vmem,
        scratch_shapes=[
            pltpu.VMEM((rows, feat), bf16),
            pltpu.VMEM((chosen, rows), jnp.int32),
            pltpu.VMEM((chosen, rows), f32),
            pltpu.VMEM((1, rows), jnp.int32),
            pltpu.VMEM((1, rows), jnp.int32),
            pltpu.VMEM((before, rows, width), bf16),
            pltpu.VMEM((horizon, width), f32),
            pltpu.VMEM(conv_weight.shape, f32),
            pltpu.VMEM((horizon, rows, width), f32),
            pltpu.VMEM((rows, horizon, width), f32),
            pltpu.VMEM((feat, hid), bf16),
            pltpu.VMEM((feat, hid), bf16),
            pltpu.VMEM((hid, feat), bf16),
            pltpu.VMEM((feat, width), bf16),
            pltpu.VMEM((every, feat + extra), bf16),
            pltpu.VMEM((every, hid), bf16),
            pltpu.VMEM((every, hid), bf16),
            pltpu.VMEM((every, feat), bf16),
            pltpu.VMEM((every // 2, feat), bf16),
            pltpu.VMEM((line * rows, feat), bf16),
            pltpu.VMEM((line * rows, feat), bf16),
            pltpu.VMEM((line * rows, feat), bf16),
            pltpu.VMEM((line * rows, feat), bf16),
            pltpu.VMEM((rows, feat), bf16),
            dma((12,)),
            dma((line + 1,)),
            dma((line,)),
            dma((line,)),
            dma((line,)),
            dma((2, line)),
            dma((2, line)),
            dma((2, cuts)),
            dma((2, cuts)),
            dma((line, cuts)),
            dma((line, cuts)),
            dma((line, cuts)),
            dma((line, cuts)),
            dma((cuts,)),
        ],
        compiler_params=pltpu.CompilerParams(
            collective_id=0, has_side_effects=True, vmem_limit_bytes=60 * 1024 * 1024
        ),
    )(
        thinker_rows,
        expert_ids.T,
        gate_weights.T,
        talker_slot,
        speech_count.reshape(1, rows),
        left_context.transpose(1, 0, 2),
        frame_offset,
        conv_weight,
        w_gate,
        w_up,
        w_down,
        talker_proj,
    )


def local(
    thinker_rows,
    expert_ids,
    gate_weights,
    w_gate,
    w_up,
    w_down,
    talker_proj,
    talker_slot,
    speech_count,
    left_context,
    frame_offset,
    conv_weight,
):
    devices = lax.axis_size("ep")
    streams_here = thinker_rows.shape[0]
    dense = streams_here <= CAP and streams_here == devices and devices == 4 * 4
    experts = (
        thinker_rows, expert_ids, gate_weights, w_gate, w_up, w_down, talker_proj, talker_slot
    )
    voices = (speech_count, left_context, frame_offset, conv_weight)
    if dense:
        return dense_path(*experts, *voices)
    return vocode(capacity_path(*experts), *voices)


def solution(mesh):
    in_specs = (
        P(("groups", "ep"), None),
        P(("groups", "ep"), None),
        P(("groups", "ep"), None),
        P("ep", None, None),
        P("ep", None, None),
        P("ep", None, None),
        P(),
        P(("groups", "ep"), None),
        P(("groups", "ep")),
        P(("groups", "ep"), None, None),
        P(),
        P(),
    )
    out_specs = P(("groups", "ep"), None, None)
    return jax.shard_map(local, mesh=mesh, in_specs=in_specs, out_specs=out_specs, check_vma=False)
```

```python
import functools

import jax
import jax.numpy as jnp
from jax import lax
from jax.experimental import pallas as pl
from jax.experimental.pallas import tpu as pltpu
from jax.sharding import PartitionSpec as P

CAP = 16
LANES = 128


def expert_block(block_rows, gate_mat, up_mat, down_mat):
    gate_act = jnp.dot(block_rows, gate_mat, preferred_element_type=jnp.float32)
    up_act = jnp.dot(block_rows, up_mat, preferred_element_type=jnp.float32)
    inner = (jax.nn.silu(gate_act) * up_act).astype(jnp.bfloat16)
    return jnp.dot(inner, down_mat, preferred_element_type=jnp.float32).astype(jnp.bfloat16)


def project(hidden, talker_proj):
    values = hidden.astype(jnp.float32)
    scaled = values * lax.rsqrt(jnp.mean(values * values, axis=-1, keepdims=True) + 1e-06)
    return jnp.dot(
        scaled.astype(jnp.bfloat16), talker_proj, preferred_element_type=jnp.float32
    ).astype(jnp.bfloat16)


def vocode(owned, speech_count, left_context, frame_offset, conv_weight):
    frames = owned.astype(jnp.float32)[:, None, :] + frame_offset[None, :, :]
    sequence = jnp.concatenate([left_context.astype(jnp.float32), frames], axis=1)
    taps = conv_weight.shape[0]
    horizon = frame_offset.shape[0]
    result = jnp.zeros_like(frames)
    for offset in range(taps):
        result = (
            result + conv_weight[offset][None, None, :] * sequence[:, offset : offset + horizon, :]
        )
    active = jnp.arange(horizon, dtype=jnp.int32)[None, :, None] < speech_count[:, None, None]
    return jnp.where(active, result, 0.0).astype(jnp.bfloat16)


def slot_positions(expert_ids, experts):
    flat_expert = expert_ids.reshape(-1)
    onehot = (flat_expert[:, None] == jnp.arange(experts, dtype=jnp.int32)[None, :]).astype(
        jnp.int32
    )
    position = jnp.sum((jnp.cumsum(onehot, axis=0) - onehot) * onehot, axis=1)
    return (flat_expert, position)


def run_and_return(buffer, w_gate, w_up, w_down):
    sources, slot_count, features = buffer.shape
    flattened = buffer.reshape(sources * slot_count, features)
    outputs = expert_block(flattened, w_gate[0], w_up[0], w_down[0]).reshape(
        sources, slot_count, features
    )
    return lax.all_to_all(outputs, "ep", split_axis=0, concat_axis=0, tiled=True)


def capacity_path(
    thinker_rows, expert_ids, gate_weights, w_gate, w_up, w_down, talker_proj, talker_slot
):
    devices = lax.axis_size("ep")
    streams_here, features = thinker_rows.shape
    chosen = expert_ids.shape[1]
    flat_expert, position = slot_positions(expert_ids, devices)
    row_index = jnp.arange(streams_here * chosen, dtype=jnp.int32) // chosen
    outgoing = (
        jnp.zeros((devices, CAP, features), jnp.bfloat16)
        .at[flat_expert, position]
        .set(thinker_rows[row_index])
    )
    returned = run_and_return(
        lax.all_to_all(outgoing, "ep", split_axis=0, concat_axis=0, tiled=True),
        w_gate,
        w_up,
        w_down,
    )
    lookup = (
        returned[flat_expert, position].astype(jnp.float32).reshape(streams_here, chosen, features)
    )
    mixture = jnp.sum(gate_weights[:, :, None] * lookup, axis=1)
    hidden = (thinker_rows.astype(jnp.float32) + mixture).astype(jnp.bfloat16)
    slots = talker_slot[0]
    per_owner = streams_here // devices
    talker_rows = project(hidden, talker_proj)
    placed = (
        jnp.zeros_like(talker_rows)
        .at[slots]
        .set(talker_rows)
        .reshape(devices, per_owner, talker_rows.shape[1])
    )
    return lax.all_to_all(placed, "ep", split_axis=0, concat_axis=0, tiled=True).reshape(
        streams_here, talker_rows.shape[1]
    )


def dense_kernel(
    n,
    rows_hbm,
    ids_hbm,
    gates_hbm,
    slot_hbm,
    count_hbm,
    context_hbm,
    offset_hbm,
    taps_hbm,
    wg_hbm,
    wu_hbm,
    wd_hbm,
    proj_hbm,
    voice_ref,
    rows_ref,
    ids_ref,
    gates_ref,
    slot_ref,
    count_ref,
    context,
    frame_offset,
    taps,
    base_voice,
    gains,
    order,
    keep,
    voices,
    wg,
    wu,
    wd,
    proj,
    x_all,
    inner,
    grouped,
    part,
    sib_in,
    pair_out,
    y_in,
    y_out,
    z_in,
    load_sem,
    gz_send,
    gz_recv,
    gy_send,
    gy_recv,
    gs_send,
    gs_recv,
    rs_send,
    rs_recv,
    ry_send,
    ry_recv,
    rz_send,
    rz_recv,
):
    f32, bf16 = jnp.float32, jnp.bfloat16
    rows, feat = rows_hbm.shape
    hid = wg.shape[1]
    width = proj.shape[1]
    line = n // 4
    half = line * rows
    tile = min(256, hid)
    me = lax.axis_index("ep")
    z = me // 4
    within = me % 4
    y = within // 2
    core = within % 2
    y_peer = me + 2 - 4 * y
    sibling = me + 1 - 2 * core

    def block(section, pos):
        return pl.ds(pl.multiple_of(section * half + pos * rows, rows), rows)

    own = block(0, z)
    loads = [
        pltpu.make_async_copy(src, dst, load_sem.at[i])
        for i, (src, dst) in enumerate(
            (
                (rows_hbm, rows_ref),
                (ids_hbm, ids_ref),
                (gates_hbm, gates_ref),
                (slot_hbm, slot_ref),
                (count_hbm, count_ref),
                (context_hbm, context),
                (offset_hbm, frame_offset),
                (taps_hbm, taps),
                (wg_hbm.at[0], wg),
                (wu_hbm.at[0], wu),
                (wd_hbm.at[0], wd),
                (proj_hbm, proj),
            )
        )
    ]
    for load in loads[:4]:
        load.start()

    z_peers = [lax.rem(z + k, line) * 4 + within for k in range(1, line)]
    partners = z_peers + [y_peer, sibling]
    barrier = pltpu.get_barrier_semaphore()
    for peer in partners:
        pl.semaphore_signal(barrier, inc=1, device_id={"ep": peer})

    extra = x_all.shape[1] - feat
    spot = lax.broadcasted_iota(jnp.int32, (extra, rows), 0)
    expert_of = lax.rem(spot, n)
    weight = jnp.zeros((extra, rows), f32)
    for load in loads[:4]:
        load.wait()
    for j in range(ids_ref.shape[0]):
        weight = weight + jnp.where(
            ids_ref[j : j + 1, :] == expert_of, gates_ref[j : j + 1, :], 0.0
        )
    high = weight.astype(bf16).astype(f32)
    mid = (weight - high).astype(bf16).astype(f32)
    low = weight - high - mid
    coded = jnp.where(spot < n, high, jnp.where(spot < 2 * n, mid, jnp.where(spot < 3 * n, low, 0.0)))
    owner = lax.broadcasted_iota(jnp.int32, (n, rows), 0)
    pick = jnp.where(owner == slot_ref[...], 1.0, 0.0).astype(bf16)
    x_all[own, :feat] = jnp.dot(pick, rows_ref[...], preferred_element_type=f32).astype(bf16)
    x_all[own, feat:] = lax.dot_general(
        pick, coded.astype(bf16), (((1,), (1,)), ((), ())), preferred_element_type=f32
    ).astype(bf16)

    pl.semaphore_wait(barrier, len(partners))

    def remote(src, dst, send, recv, peer):
        return pltpu.make_async_remote_copy(
            src_ref=src, dst_ref=dst, send_sem=send, recv_sem=recv, device_id={"ep": peer}
        )

    def place(index):
        section = index // half
        device = (
            (index % half) // rows * 4
            + jnp.where(section // 2 == 0, y, 1 - y) * 2
            + jnp.where(section % 2 == 0, core, 1 - core)
        )
        return device, index % rows

    def regroup():
        every = n * rows
        row_owner, row_source = place(lax.broadcasted_iota(jnp.int32, (every, 1), 0))
        col_source, col_owner = place(lax.broadcasted_iota(jnp.int32, (1, every), 1))
        match = (row_owner == col_owner) & (row_source == col_source)
        return jnp.where(match, 1.0, 0.0).astype(bf16)

    def owned_rows():
        col_source, col_owner = place(lax.broadcasted_iota(jnp.int32, (1, n * rows), 1))
        source = lax.broadcasted_iota(jnp.int32, (rows, 1), 0)
        return jnp.where((col_source == source) & (col_owner == me), 1.0, 0.0).astype(bf16)

    def z_copy(peer, src):
        here = x_all.at[block(0, src)]
        return remote(here, here, gz_send.at[peer], gz_recv.at[src], peer * 4 + within)

    def y_copy(src):
        return remote(
            x_all.at[block(0, src)],
            x_all.at[block(2, src)],
            gy_send.at[src],
            gy_recv.at[src],
            y_peer,
        )

    def s_copy(section, src):
        return remote(
            x_all.at[block(2 * section, src)],
            x_all.at[block(2 * section + 1, src)],
            gs_send.at[section, src],
            gs_recv.at[section, src],
            sibling,
        )

    def at_distance(d, use):
        for src in (z,) if d == 0 else (z - d, z + d):
            pl.when((src >= 0) & (src < line))(functools.partial(use, src))

    def to_z(d, act):
        at_distance(d, lambda peer: act(z_copy(peer, z)))

    def from_z(d):
        at_distance(d, lambda src: z_copy(src, src).wait_recv())

    def hand_on(src):
        y_copy(src).start()
        s_copy(0, src).start()

    def from_y(src):
        y_copy(src).wait_recv()
        s_copy(1, src).start()

    to_z(1, lambda copy: copy.start())
    hand_on(z)
    for d in range(2, line):
        to_z(d, lambda copy: copy.start())
    for load in loads[4:]:
        load.start()

    order[...] = regroup()
    keep[...] = owned_rows()

    for d in range(1, line):
        from_z(d)
        at_distance(d, hand_on)
        if d < line - 1:
            at_distance(d - 1, from_y)

    loads[8].wait()
    loads[9].wait()

    def up_pass(base, first, stop):
        span = pl.ds(base, 2 * half)
        lanes = lax.broadcasted_iota(jnp.int32, (2 * half, extra), 1)
        mine = (lax.rem(lanes, n) == me) & (lanes < 3 * n)
        coef = jnp.sum(
            jnp.where(mine, x_all[span, feat:].astype(f32), 0.0), axis=1, keepdims=True
        )

        def step(j, carry):
            cols = pl.ds(pl.multiple_of(j * tile, tile), tile)
            x = x_all[span, :feat]
            gate_act = jnp.dot(x, wg[:, cols], preferred_element_type=f32)
            up_act = jnp.dot(x, wu[:, cols], preferred_element_type=f32)
            inner[span, cols] = (jax.nn.silu(gate_act) * up_act * coef).astype(bf16)
            return carry

        lax.fori_loop(first, stop, step, 0)

    def down_pass(base, cut):
        span = pl.ds(base, 2 * half)

        def step(j, carry):
            cols = pl.ds(pl.multiple_of(cut * piece + j * tile, tile), tile)
            out = jnp.dot(grouped[span, :], wd[:, cols], preferred_element_type=f32)
            part[span, cols] = out.astype(bf16)
            return carry

        lax.fori_loop(0, piece // tile, step, 0)

    cuts = rs_send.shape[1]
    piece = feat // cuts

    def columns(cut):
        return pl.ds(cut * piece, piece)

    reduce_s = [
        [
            remote(
                part.at[pl.ds((2 * section + 1) * half, half), columns(cut)],
                sib_in.at[pl.ds(section * half, half), columns(cut)],
                rs_send.at[section, cut],
                rs_recv.at[section, cut],
                sibling,
            )
            for cut in range(cuts)
        ]
        for section in range(2)
    ]
    for src in range(line):
        s_copy(0, src).wait_recv()
    steps = hid // tile
    up_pass(0, 0, steps // 2)
    for d in range(max(line - 2, 0), line):
        at_distance(d, from_y)
    up_pass(0, steps // 2, steps)
    for src in range(line):
        s_copy(1, src).wait_recv()
    up_pass(2 * half, 0, steps)
    grouped[...] = jnp.dot(order[...], inner[...], preferred_element_type=f32).astype(bf16)
    loads[10].wait()
    for cut in range(cuts):
        down_pass(2 * half, cut)
        reduce_s[1][cut].start()

    def target(k):
        return lax.rem(z + k, line)

    reduce_y = [
        [
            remote(
                pair_out.at[block(0, target(k)), columns(cut)],
                y_in.at[block(0, target(k)), columns(cut)],
                ry_send.at[k, cut],
                ry_recv.at[k, cut],
                y_peer,
            )
            for cut in range(cuts)
        ]
        for k in range(line)
    ]
    reduce_z = [
        [
            remote(
                y_out.at[block(0, target(k)), columns(cut)],
                z_in.at[block(0, k), columns(cut)],
                rz_send.at[k, cut],
                rz_recv.at[k, cut],
                target(k) * 4 + within,
            )
            for cut in range(cuts)
        ]
        for k in range(1, line)
    ]

    def to_y(k, cut):
        cols = columns(cut)
        mine, theirs = block(2, target(k)), block(1, target(k))
        pair_out[block(0, target(k)), cols] = (
            part[mine, cols].astype(f32) + sib_in[theirs, cols].astype(f32)
        ).astype(bf16)
        reduce_y[k][cut].start()

    for cut in range(cuts):
        down_pass(0, cut)
        reduce_s[0][cut].start()
        reduce_s[1][cut].wait_recv()
        for k in range(1, line):
            to_y(k, cut)
    for cut in range(cuts):
        to_y(0, cut)
    for cut in range(cuts):
        cols = columns(cut)
        reduce_s[0][cut].wait_recv()
        for k in range(1, line):
            here = block(0, target(k))
            reduce_y[k][cut].wait_recv()
            y_out[here, cols] = (
                part[here, cols].astype(f32)
                + sib_in[here, cols].astype(f32)
                + y_in[here, cols].astype(f32)
            ).astype(bf16)
            reduce_z[k - 1][cut].start()
    for load in loads[4:8]:
        load.wait()
    before = context.shape[0]
    horizon = frame_offset.shape[0]
    for f in range(horizon):
        voice = jnp.zeros((rows, width), f32)
        for t in range(taps.shape[0]):
            tap = taps[t : t + 1, :]
            if f + t < before:
                voice = voice + tap * context[f + t].astype(f32)
            else:
                voice = voice + tap * frame_offset[f + t - before : f + t - before + 1, :]
        base_voice[f] = voice
        gains[f : f + 1, :] = jnp.sum(taps[before - f :, :], axis=0, keepdims=True)

    diagonal = lax.broadcasted_iota(jnp.int32, (rows, rows), 0) == lax.broadcasted_iota(
        jnp.int32, (rows, rows), 1
    )
    count = jnp.sum(
        jnp.where(diagonal, count_ref[...].astype(f32), 0.0), axis=1, keepdims=True
    )
    residual = jnp.dot(keep[...], x_all[:, :feat], preferred_element_type=f32)
    for cut in range(cuts):
        reduce_y[0][cut].wait_recv()
    total = (
        residual
        + part[own, :].astype(f32)
        + sib_in[own, :].astype(f32)
        + y_in[own, :].astype(f32)
    )
    for k in range(1, line):
        for cut in range(cuts):
            reduce_z[k - 1][cut].wait_recv()
        total = total + z_in[k * rows : (k + 1) * rows, :].astype(f32)
    hidden = total.astype(bf16).astype(f32)
    scale = lax.rsqrt(jnp.mean(hidden * hidden, axis=-1, keepdims=True) + 1e-06)
    normed = (hidden * scale).astype(bf16)

    loads[11].wait()
    for j in range(width // tile):
        cols = slice(j * tile, (j + 1) * tile)
        talk = jnp.dot(normed, proj[:, cols], preferred_element_type=f32)
        owned = talk.astype(bf16).astype(f32)
        for f in range(horizon):
            voice = base_voice[f, :, cols] + gains[f : f + 1, cols] * owned
            voices[:, f, cols] = jnp.where(count > f, voice, 0.0)
        voice_ref[:, :, cols] = voices[:, :, cols].astype(bf16)

    for d in range(1, line):
        to_z(d, lambda copy: copy.wait_send())
    for src in range(line):
        y_copy(src).wait_send()
        s_copy(0, src).wait_send()
        s_copy(1, src).wait_send()
    for group in reduce_s + reduce_y + reduce_z:
        for copy in group:
            copy.wait_send()


def dense_path(
    thinker_rows,
    expert_ids,
    gate_weights,
    w_gate,
    w_up,
    w_down,
    talker_proj,
    talker_slot,
    speech_count,
    left_context,
    frame_offset,
    conv_weight,
):
    n = lax.axis_size("ep")
    rows, feat = thinker_rows.shape
    hid = w_gate.shape[2]
    width = talker_proj.shape[1]
    line = n // 4
    every = n * rows
    extra = -(-3 * n // LANES) * LANES
    bf16, f32 = jnp.bfloat16, jnp.float32
    chosen = expert_ids.shape[1]
    before = left_context.shape[1]
    horizon = frame_offset.shape[0]
    cuts = 2
    vmem = pl.BlockSpec(memory_space=pltpu.VMEM)
    hbm = pl.BlockSpec(memory_space=pl.ANY)
    dma = pltpu.SemaphoreType.DMA
    return pl.pallas_call(
        functools.partial(dense_kernel, n),
        out_shape=jax.ShapeDtypeStruct((rows, horizon, width), bf16),
        in_specs=[hbm] * 12,
        out_specs=vmem,
        scratch_shapes=[
            pltpu.VMEM((rows, feat), bf16),
            pltpu.VMEM((chosen, rows), jnp.int32),
            pltpu.VMEM((chosen, rows), f32),
            pltpu.VMEM((1, rows), jnp.int32),
            pltpu.VMEM((1, rows), jnp.int32),
            pltpu.VMEM((before, rows, width), bf16),
            pltpu.VMEM((horizon, width), f32),
            pltpu.VMEM(conv_weight.shape, f32),
            pltpu.VMEM((horizon, rows, width), f32),
            pltpu.VMEM((horizon, width), f32),
            pltpu.VMEM((every, every), bf16),
            pltpu.VMEM((rows, every), bf16),
            pltpu.VMEM((rows, horizon, width), f32),
            pltpu.VMEM((feat, hid), bf16),
            pltpu.VMEM((feat, hid), bf16),
            pltpu.VMEM((hid, feat), bf16),
            pltpu.VMEM((feat, width), bf16),
            pltpu.VMEM((every, feat + extra), bf16),
            pltpu.VMEM((every, hid), bf16),
            pltpu.VMEM((every, hid), bf16),
            pltpu.VMEM((every, feat), bf16),
            pltpu.VMEM((every // 2, feat), bf16),
            pltpu.VMEM((line * rows, feat), bf16),
            pltpu.VMEM((line * rows, feat), bf16),
            pltpu.VMEM((line * rows, feat), bf16),
            pltpu.VMEM((line * rows, feat), bf16),
            dma((12,)),
            dma((line,)),
            dma((line,)),
            dma((line,)),
            dma((line,)),
            dma((2, line)),
            dma((2, line)),
            dma((2, cuts)),
            dma((2, cuts)),
            dma((line, cuts)),
            dma((line, cuts)),
            dma((line, cuts)),
            dma((line, cuts)),
        ],
        compiler_params=pltpu.CompilerParams(
            collective_id=0, has_side_effects=True, vmem_limit_bytes=60 * 1024 * 1024
        ),
    )(
        thinker_rows,
        expert_ids.T,
        gate_weights.T,
        talker_slot,
        speech_count.reshape(1, rows),
        left_context.transpose(1, 0, 2),
        frame_offset,
        conv_weight,
        w_gate,
        w_up,
        w_down,
        talker_proj,
    )


def local(
    thinker_rows,
    expert_ids,
    gate_weights,
    w_gate,
    w_up,
    w_down,
    talker_proj,
    talker_slot,
    speech_count,
    left_context,
    frame_offset,
    conv_weight,
):
    devices = lax.axis_size("ep")
    streams_here = thinker_rows.shape[0]
    dense = streams_here <= CAP and streams_here == devices and devices % 4 == 0
    experts = (
        thinker_rows, expert_ids, gate_weights, w_gate, w_up, w_down, talker_proj, talker_slot
    )
    voices = (speech_count, left_context, frame_offset, conv_weight)
    if dense:
        return dense_path(*experts, *voices)
    return vocode(capacity_path(*experts), *voices)


def solution(mesh):
    in_specs = (
        P(("groups", "ep"), None),
        P(("groups", "ep"), None),
        P(("groups", "ep"), None),
        P("ep", None, None),
        P("ep", None, None),
        P("ep", None, None),
        P(),
        P(("groups", "ep"), None),
        P(("groups", "ep")),
        P(("groups", "ep"), None, None),
        P(),
        P(),
    )
    out_specs = P(("groups", "ep"), None, None)
    return jax.shard_map(local, mesh=mesh, in_specs=in_specs, out_specs=out_specs, check_vma=False)
```

```python
import functools

import jax
import jax.numpy as jnp
from jax import lax
from jax.experimental import pallas as pl
from jax.experimental.pallas import tpu as pltpu
from jax.sharding import PartitionSpec as P

CAP = 16
LANES = 128


def expert_block(block_rows, gate_mat, up_mat, down_mat):
    gate_act = jnp.dot(block_rows, gate_mat, preferred_element_type=jnp.float32)
    up_act = jnp.dot(block_rows, up_mat, preferred_element_type=jnp.float32)
    inner = (jax.nn.silu(gate_act) * up_act).astype(jnp.bfloat16)
    return jnp.dot(inner, down_mat, preferred_element_type=jnp.float32).astype(jnp.bfloat16)


def project(hidden, talker_proj):
    values = hidden.astype(jnp.float32)
    scaled = values * lax.rsqrt(jnp.mean(values * values, axis=-1, keepdims=True) + 1e-06)
    return jnp.dot(
        scaled.astype(jnp.bfloat16), talker_proj, preferred_element_type=jnp.float32
    ).astype(jnp.bfloat16)


def vocode(owned, speech_count, left_context, frame_offset, conv_weight):
    frames = owned.astype(jnp.float32)[:, None, :] + frame_offset[None, :, :]
    sequence = jnp.concatenate([left_context.astype(jnp.float32), frames], axis=1)
    taps = conv_weight.shape[0]
    horizon = frame_offset.shape[0]
    result = jnp.zeros_like(frames)
    for offset in range(taps):
        result = (
            result + conv_weight[offset][None, None, :] * sequence[:, offset : offset + horizon, :]
        )
    active = jnp.arange(horizon, dtype=jnp.int32)[None, :, None] < speech_count[:, None, None]
    return jnp.where(active, result, 0.0).astype(jnp.bfloat16)


def slot_positions(expert_ids, experts):
    flat_expert = expert_ids.reshape(-1)
    onehot = (flat_expert[:, None] == jnp.arange(experts, dtype=jnp.int32)[None, :]).astype(
        jnp.int32
    )
    position = jnp.sum((jnp.cumsum(onehot, axis=0) - onehot) * onehot, axis=1)
    return (flat_expert, position)


def run_and_return(buffer, w_gate, w_up, w_down):
    sources, slot_count, features = buffer.shape
    flattened = buffer.reshape(sources * slot_count, features)
    outputs = expert_block(flattened, w_gate[0], w_up[0], w_down[0]).reshape(
        sources, slot_count, features
    )
    return lax.all_to_all(outputs, "ep", split_axis=0, concat_axis=0, tiled=True)


def capacity_path(
    thinker_rows, expert_ids, gate_weights, w_gate, w_up, w_down, talker_proj, talker_slot
):
    devices = lax.axis_size("ep")
    streams_here, features = thinker_rows.shape
    chosen = expert_ids.shape[1]
    flat_expert, position = slot_positions(expert_ids, devices)
    row_index = jnp.arange(streams_here * chosen, dtype=jnp.int32) // chosen
    outgoing = (
        jnp.zeros((devices, CAP, features), jnp.bfloat16)
        .at[flat_expert, position]
        .set(thinker_rows[row_index])
    )
    returned = run_and_return(
        lax.all_to_all(outgoing, "ep", split_axis=0, concat_axis=0, tiled=True),
        w_gate,
        w_up,
        w_down,
    )
    lookup = (
        returned[flat_expert, position].astype(jnp.float32).reshape(streams_here, chosen, features)
    )
    mixture = jnp.sum(gate_weights[:, :, None] * lookup, axis=1)
    hidden = (thinker_rows.astype(jnp.float32) + mixture).astype(jnp.bfloat16)
    slots = talker_slot[0]
    per_owner = streams_here // devices
    talker_rows = project(hidden, talker_proj)
    placed = (
        jnp.zeros_like(talker_rows)
        .at[slots]
        .set(talker_rows)
        .reshape(devices, per_owner, talker_rows.shape[1])
    )
    return lax.all_to_all(placed, "ep", split_axis=0, concat_axis=0, tiled=True).reshape(
        streams_here, talker_rows.shape[1]
    )


def dense_kernel(
    n,
    rows_hbm,
    ids_hbm,
    gates_hbm,
    slot_hbm,
    count_hbm,
    context_hbm,
    offset_hbm,
    taps_hbm,
    wg_hbm,
    wu_hbm,
    wd_hbm,
    proj_hbm,
    voice_ref,
    rows_ref,
    ids_ref,
    gates_ref,
    slot_ref,
    count_ref,
    context,
    frame_offset,
    taps,
    base_voice,
    gains,
    order,
    keep,
    voices,
    wg,
    wu,
    wd,
    proj,
    x_all,
    inner,
    grouped,
    part,
    sib_in,
    pair_out,
    y_in,
    y_out,
    z_in,
    load_sem,
    gz_send,
    gz_recv,
    gy_send,
    gy_recv,
    gs_send,
    gs_recv,
    rs_send,
    rs_recv,
    ry_send,
    ry_recv,
    rz_send,
    rz_recv,
):
    f32, bf16 = jnp.float32, jnp.bfloat16
    rows, feat = rows_hbm.shape
    hid = wg.shape[1]
    width = proj.shape[1]
    line = n // 4
    half = line * rows
    tile = min(256, hid)
    me = lax.axis_index("ep")
    z = me // 4
    within = me % 4
    y = within // 2
    core = within % 2
    y_peer = me + 2 - 4 * y
    sibling = me + 1 - 2 * core

    def block(section, pos):
        return pl.ds(pl.multiple_of(section * half + pos * rows, rows), rows)

    own = block(0, z)
    loads = [
        pltpu.make_async_copy(src, dst, load_sem.at[i])
        for i, (src, dst) in enumerate(
            (
                (rows_hbm, rows_ref),
                (ids_hbm, ids_ref),
                (gates_hbm, gates_ref),
                (slot_hbm, slot_ref),
                (count_hbm, count_ref),
                (context_hbm, context),
                (offset_hbm, frame_offset),
                (taps_hbm, taps),
                (wg_hbm.at[0], wg),
                (wu_hbm.at[0], wu),
                (wd_hbm.at[0], wd),
                (proj_hbm, proj),
            )
        )
    ]
    for load in loads[:4]:
        load.start()

    z_peers = [lax.rem(z + k, line) * 4 + within for k in range(1, line)]
    partners = z_peers + [y_peer, sibling]
    barrier = pltpu.get_barrier_semaphore()
    for peer in partners:
        pl.semaphore_signal(barrier, inc=1, device_id={"ep": peer})

    for load in loads[8:10]:
        load.start()

    extra = x_all.shape[1] - feat
    spot = lax.broadcasted_iota(jnp.int32, (extra, rows), 0)
    expert_of = lax.rem(spot, n)
    weight = jnp.zeros((extra, rows), f32)
    for load in loads[:4]:
        load.wait()
    for j in range(ids_ref.shape[0]):
        weight = weight + jnp.where(
            ids_ref[j : j + 1, :] == expert_of, gates_ref[j : j + 1, :], 0.0
        )
    high = weight.astype(bf16).astype(f32)
    mid = (weight - high).astype(bf16).astype(f32)
    low = weight - high - mid
    coded = jnp.where(spot < n, high, jnp.where(spot < 2 * n, mid, jnp.where(spot < 3 * n, low, 0.0)))
    owner = lax.broadcasted_iota(jnp.int32, (n, rows), 0)
    pick = jnp.where(owner == slot_ref[...], 1.0, 0.0).astype(bf16)
    x_all[own, :feat] = jnp.dot(pick, rows_ref[...], preferred_element_type=f32).astype(bf16)
    x_all[own, feat:] = lax.dot_general(
        pick, coded.astype(bf16), (((1,), (1,)), ((), ())), preferred_element_type=f32
    ).astype(bf16)

    pl.semaphore_wait(barrier, len(partners))

    def remote(src, dst, send, recv, peer):
        return pltpu.make_async_remote_copy(
            src_ref=src, dst_ref=dst, send_sem=send, recv_sem=recv, device_id={"ep": peer}
        )

    def place(index):
        section = index // half
        device = (
            (index % half) // rows * 4
            + jnp.where(section // 2 == 0, y, 1 - y) * 2
            + jnp.where(section % 2 == 0, core, 1 - core)
        )
        return device, index % rows

    def regroup():
        every = n * rows
        row_owner, row_source = place(lax.broadcasted_iota(jnp.int32, (every, 1), 0))
        col_source, col_owner = place(lax.broadcasted_iota(jnp.int32, (1, every), 1))
        match = (row_owner == col_owner) & (row_source == col_source)
        return jnp.where(match, 1.0, 0.0).astype(bf16)

    def owned_rows():
        col_source, col_owner = place(lax.broadcasted_iota(jnp.int32, (1, n * rows), 1))
        source = lax.broadcasted_iota(jnp.int32, (rows, 1), 0)
        return jnp.where((col_source == source) & (col_owner == me), 1.0, 0.0).astype(bf16)

    def z_copy(peer, src):
        here = x_all.at[block(0, src)]
        return remote(here, here, gz_send.at[peer], gz_recv.at[src], peer * 4 + within)

    def y_copy(src):
        return remote(
            x_all.at[block(0, src)],
            x_all.at[block(2, src)],
            gy_send.at[src],
            gy_recv.at[src],
            y_peer,
        )

    def s_copy(section, src):
        return remote(
            x_all.at[block(2 * section, src)],
            x_all.at[block(2 * section + 1, src)],
            gs_send.at[section, src],
            gs_recv.at[section, src],
            sibling,
        )

    def at_distance(d, use):
        for src in (z,) if d == 0 else (z - d, z + d):
            pl.when((src >= 0) & (src < line))(functools.partial(use, src))

    def to_z(d, act):
        at_distance(d, lambda peer: act(z_copy(peer, z)))

    def from_z(d):
        at_distance(d, lambda src: z_copy(src, src).wait_recv())

    def hand_on(src):
        y_copy(src).start()
        s_copy(0, src).start()

    def from_y(src):
        y_copy(src).wait_recv()
        s_copy(1, src).start()

    to_z(1, lambda copy: copy.start())
    hand_on(z)
    for d in range(2, line):
        to_z(d, lambda copy: copy.start())
    for load in loads[4:8]:
        load.start()

    order[...] = regroup()
    keep[...] = owned_rows()

    for d in range(1, line):
        from_z(d)
        at_distance(d, hand_on)
        if d < line - 1:
            at_distance(d - 1, from_y)

    loads[10].start()
    loads[8].wait()
    loads[9].wait()

    def up_pass(base, first, stop):
        span = pl.ds(base, 2 * half)
        lanes = lax.broadcasted_iota(jnp.int32, (2 * half, extra), 1)
        mine = (lax.rem(lanes, n) == me) & (lanes < 3 * n)
        coef = jnp.sum(
            jnp.where(mine, x_all[span, feat:].astype(f32), 0.0), axis=1, keepdims=True
        )

        def step(j, carry):
            cols = pl.ds(pl.multiple_of(j * tile, tile), tile)
            x = x_all[span, :feat]
            gate_act = jnp.dot(x, wg[:, cols], preferred_element_type=f32)
            up_act = jnp.dot(x, wu[:, cols], preferred_element_type=f32)
            inner[span, cols] = (jax.nn.silu(gate_act) * up_act * coef).astype(bf16)
            return carry

        lax.fori_loop(first, stop, step, 0)

    def down_pass(base, cut):
        span = pl.ds(base, 2 * half)

        def step(j, carry):
            cols = pl.ds(pl.multiple_of(cut * piece + j * tile, tile), tile)
            out = jnp.dot(grouped[span, :], wd[:, cols], preferred_element_type=f32)
            part[span, cols] = out.astype(bf16)
            return carry

        lax.fori_loop(0, piece // tile, step, 0)

    cuts = rs_send.shape[1]
    piece = feat // cuts

    def columns(cut):
        return pl.ds(cut * piece, piece)

    reduce_s = [
        [
            remote(
                part.at[pl.ds((2 * section + 1) * half, half), columns(cut)],
                sib_in.at[pl.ds(section * half, half), columns(cut)],
                rs_send.at[section, cut],
                rs_recv.at[section, cut],
                sibling,
            )
            for cut in range(cuts)
        ]
        for section in range(2)
    ]
    for src in range(line):
        s_copy(0, src).wait_recv()
    steps = hid // tile
    up_pass(0, 0, steps // 2)
    for d in range(max(line - 2, 0), line):
        at_distance(d, from_y)
    up_pass(0, steps // 2, steps)
    for src in range(line):
        s_copy(1, src).wait_recv()
    up_pass(2 * half, 0, steps)
    grouped[...] = jnp.dot(order[...], inner[...], preferred_element_type=f32).astype(bf16)
    loads[10].wait()
    loads[11].start()
    for cut in range(cuts):
        down_pass(2 * half, cut)
        reduce_s[1][cut].start()

    def target(k):
        return lax.rem(z + k, line)

    reduce_y = [
        [
            remote(
                pair_out.at[block(0, target(k)), columns(cut)],
                y_in.at[block(0, target(k)), columns(cut)],
                ry_send.at[k, cut],
                ry_recv.at[k, cut],
                y_peer,
            )
            for cut in range(cuts)
        ]
        for k in range(line)
    ]
    reduce_z = [
        [
            remote(
                y_out.at[block(0, target(k)), columns(cut)],
                z_in.at[block(0, k), columns(cut)],
                rz_send.at[k, cut],
                rz_recv.at[k, cut],
                target(k) * 4 + within,
            )
            for cut in range(cuts)
        ]
        for k in range(1, line)
    ]

    def to_y(k, cut):
        cols = columns(cut)
        mine, theirs = block(2, target(k)), block(1, target(k))
        pair_out[block(0, target(k)), cols] = (
            part[mine, cols].astype(f32) + sib_in[theirs, cols].astype(f32)
        ).astype(bf16)
        reduce_y[k][cut].start()

    for cut in range(cuts):
        down_pass(0, cut)
        reduce_s[0][cut].start()
        reduce_s[1][cut].wait_recv()
        for k in range(1, line):
            to_y(k, cut)
    for cut in range(cuts):
        to_y(0, cut)
    for cut in range(cuts):
        cols = columns(cut)
        reduce_s[0][cut].wait_recv()
        for k in range(1, line):
            here = block(0, target(k))
            reduce_y[k][cut].wait_recv()
            y_out[here, cols] = (
                part[here, cols].astype(f32)
                + sib_in[here, cols].astype(f32)
                + y_in[here, cols].astype(f32)
            ).astype(bf16)
            reduce_z[k - 1][cut].start()
    for load in loads[4:8]:
        load.wait()
    before = context.shape[0]
    horizon = frame_offset.shape[0]
    for f in range(horizon):
        voice = jnp.zeros((rows, width), f32)
        for t in range(taps.shape[0]):
            tap = taps[t : t + 1, :]
            if f + t < before:
                voice = voice + tap * context[f + t].astype(f32)
            else:
                voice = voice + tap * frame_offset[f + t - before : f + t - before + 1, :]
        base_voice[f] = voice
        gains[f : f + 1, :] = jnp.sum(taps[before - f :, :], axis=0, keepdims=True)

    diagonal = lax.broadcasted_iota(jnp.int32, (rows, rows), 0) == lax.broadcasted_iota(
        jnp.int32, (rows, rows), 1
    )
    count = jnp.sum(
        jnp.where(diagonal, count_ref[...].astype(f32), 0.0), axis=1, keepdims=True
    )
    residual = jnp.dot(keep[...], x_all[:, :feat], preferred_element_type=f32)
    for cut in range(cuts):
        reduce_y[0][cut].wait_recv()
    total = (
        residual
        + part[own, :].astype(f32)
        + sib_in[own, :].astype(f32)
        + y_in[own, :].astype(f32)
    )
    for k in range(1, line):
        for cut in range(cuts):
            reduce_z[k - 1][cut].wait_recv()
        total = total + z_in[k * rows : (k + 1) * rows, :].astype(f32)
    hidden = total.astype(bf16).astype(f32)
    scale = lax.rsqrt(jnp.mean(hidden * hidden, axis=-1, keepdims=True) + 1e-06)
    normed = (hidden * scale).astype(bf16)

    loads[11].wait()
    for j in range(width // tile):
        cols = slice(j * tile, (j + 1) * tile)
        talk = jnp.dot(normed, proj[:, cols], preferred_element_type=f32)
        owned = talk.astype(bf16).astype(f32)
        for f in range(horizon):
            voice = base_voice[f, :, cols] + gains[f : f + 1, cols] * owned
            voices[:, f, cols] = jnp.where(count > f, voice, 0.0)
        voice_ref[:, :, cols] = voices[:, :, cols].astype(bf16)

    for d in range(1, line):
        to_z(d, lambda copy: copy.wait_send())
    for src in range(line):
        y_copy(src).wait_send()
        s_copy(0, src).wait_send()
        s_copy(1, src).wait_send()
    for group in reduce_s + reduce_y + reduce_z:
        for copy in group:
            copy.wait_send()


def dense_path(
    thinker_rows,
    expert_ids,
    gate_weights,
    w_gate,
    w_up,
    w_down,
    talker_proj,
    talker_slot,
    speech_count,
    left_context,
    frame_offset,
    conv_weight,
):
    n = lax.axis_size("ep")
    rows, feat = thinker_rows.shape
    hid = w_gate.shape[2]
    width = talker_proj.shape[1]
    line = n // 4
    every = n * rows
    extra = -(-3 * n // LANES) * LANES
    bf16, f32 = jnp.bfloat16, jnp.float32
    chosen = expert_ids.shape[1]
    before = left_context.shape[1]
    horizon = frame_offset.shape[0]
    cuts = 2
    vmem = pl.BlockSpec(memory_space=pltpu.VMEM)
    hbm = pl.BlockSpec(memory_space=pl.ANY)
    dma = pltpu.SemaphoreType.DMA
    return pl.pallas_call(
        functools.partial(dense_kernel, n),
        out_shape=jax.ShapeDtypeStruct((rows, horizon, width), bf16),
        in_specs=[hbm] * 12,
        out_specs=vmem,
        scratch_shapes=[
            pltpu.VMEM((rows, feat), bf16),
            pltpu.VMEM((chosen, rows), jnp.int32),
            pltpu.VMEM((chosen, rows), f32),
            pltpu.VMEM((1, rows), jnp.int32),
            pltpu.VMEM((1, rows), jnp.int32),
            pltpu.VMEM((before, rows, width), bf16),
            pltpu.VMEM((horizon, width), f32),
            pltpu.VMEM(conv_weight.shape, f32),
            pltpu.VMEM((horizon, rows, width), f32),
            pltpu.VMEM((horizon, width), f32),
            pltpu.VMEM((every, every), bf16),
            pltpu.VMEM((rows, every), bf16),
            pltpu.VMEM((rows, horizon, width), f32),
            pltpu.VMEM((feat, hid), bf16),
            pltpu.VMEM((feat, hid), bf16),
            pltpu.VMEM((hid, feat), bf16),
            pltpu.VMEM((feat, width), bf16),
            pltpu.VMEM((every, feat + extra), bf16),
            pltpu.VMEM((every, hid), bf16),
            pltpu.VMEM((every, hid), bf16),
            pltpu.VMEM((every, feat), bf16),
            pltpu.VMEM((every // 2, feat), bf16),
            pltpu.VMEM((line * rows, feat), bf16),
            pltpu.VMEM((line * rows, feat), bf16),
            pltpu.VMEM((line * rows, feat), bf16),
            pltpu.VMEM((line * rows, feat), bf16),
            dma((12,)),
            dma((line,)),
            dma((line,)),
            dma((line,)),
            dma((line,)),
            dma((2, line)),
            dma((2, line)),
            dma((2, cuts)),
            dma((2, cuts)),
            dma((line, cuts)),
            dma((line, cuts)),
            dma((line, cuts)),
            dma((line, cuts)),
        ],
        compiler_params=pltpu.CompilerParams(
            collective_id=0, has_side_effects=True, vmem_limit_bytes=60 * 1024 * 1024
        ),
    )(
        thinker_rows,
        expert_ids.T,
        gate_weights.T,
        talker_slot,
        speech_count.reshape(1, rows),
        left_context.transpose(1, 0, 2),
        frame_offset,
        conv_weight,
        w_gate,
        w_up,
        w_down,
        talker_proj,
    )


def local(
    thinker_rows,
    expert_ids,
    gate_weights,
    w_gate,
    w_up,
    w_down,
    talker_proj,
    talker_slot,
    speech_count,
    left_context,
    frame_offset,
    conv_weight,
):
    devices = lax.axis_size("ep")
    streams_here = thinker_rows.shape[0]
    dense = streams_here <= CAP and streams_here == devices and devices % 4 == 0
    experts = (
        thinker_rows, expert_ids, gate_weights, w_gate, w_up, w_down, talker_proj, talker_slot
    )
    voices = (speech_count, left_context, frame_offset, conv_weight)
    if dense:
        return dense_path(*experts, *voices)
    return vocode(capacity_path(*experts), *voices)


def solution(mesh):
    in_specs = (
        P(("groups", "ep"), None),
        P(("groups", "ep"), None),
        P(("groups", "ep"), None),
        P("ep", None, None),
        P("ep", None, None),
        P("ep", None, None),
        P(),
        P(("groups", "ep"), None),
        P(("groups", "ep")),
        P(("groups", "ep"), None, None),
        P(),
        P(),
    )
    out_specs = P(("groups", "ep"), None, None)
    return jax.shard_map(local, mesh=mesh, in_specs=in_specs, out_specs=out_specs, check_vma=False)
```

```python
import functools

import jax
import jax.numpy as jnp
from jax import lax
from jax.experimental import pallas as pl
from jax.experimental.pallas import tpu as pltpu
from jax.sharding import PartitionSpec as P

CAP = 16
LANES = 128


def expert_block(block_rows, gate_mat, up_mat, down_mat):
    gate_act = jnp.dot(block_rows, gate_mat, preferred_element_type=jnp.float32)
    up_act = jnp.dot(block_rows, up_mat, preferred_element_type=jnp.float32)
    inner = (jax.nn.silu(gate_act) * up_act).astype(jnp.bfloat16)
    return jnp.dot(inner, down_mat, preferred_element_type=jnp.float32).astype(jnp.bfloat16)


def project(hidden, talker_proj):
    values = hidden.astype(jnp.float32)
    scaled = values * lax.rsqrt(jnp.mean(values * values, axis=-1, keepdims=True) + 1e-06)
    return jnp.dot(
        scaled.astype(jnp.bfloat16), talker_proj, preferred_element_type=jnp.float32
    ).astype(jnp.bfloat16)


def vocode(owned, speech_count, left_context, frame_offset, conv_weight):
    frames = owned.astype(jnp.float32)[:, None, :] + frame_offset[None, :, :]
    sequence = jnp.concatenate([left_context.astype(jnp.float32), frames], axis=1)
    taps = conv_weight.shape[0]
    horizon = frame_offset.shape[0]
    result = jnp.zeros_like(frames)
    for offset in range(taps):
        result = (
            result + conv_weight[offset][None, None, :] * sequence[:, offset : offset + horizon, :]
        )
    active = jnp.arange(horizon, dtype=jnp.int32)[None, :, None] < speech_count[:, None, None]
    return jnp.where(active, result, 0.0).astype(jnp.bfloat16)


def slot_positions(expert_ids, experts):
    flat_expert = expert_ids.reshape(-1)
    onehot = (flat_expert[:, None] == jnp.arange(experts, dtype=jnp.int32)[None, :]).astype(
        jnp.int32
    )
    position = jnp.sum((jnp.cumsum(onehot, axis=0) - onehot) * onehot, axis=1)
    return (flat_expert, position)


def run_and_return(buffer, w_gate, w_up, w_down):
    sources, slot_count, features = buffer.shape
    flattened = buffer.reshape(sources * slot_count, features)
    outputs = expert_block(flattened, w_gate[0], w_up[0], w_down[0]).reshape(
        sources, slot_count, features
    )
    return lax.all_to_all(outputs, "ep", split_axis=0, concat_axis=0, tiled=True)


def capacity_path(
    thinker_rows, expert_ids, gate_weights, w_gate, w_up, w_down, talker_proj, talker_slot
):
    devices = lax.axis_size("ep")
    streams_here, features = thinker_rows.shape
    chosen = expert_ids.shape[1]
    flat_expert, position = slot_positions(expert_ids, devices)
    row_index = jnp.arange(streams_here * chosen, dtype=jnp.int32) // chosen
    outgoing = (
        jnp.zeros((devices, CAP, features), jnp.bfloat16)
        .at[flat_expert, position]
        .set(thinker_rows[row_index])
    )
    returned = run_and_return(
        lax.all_to_all(outgoing, "ep", split_axis=0, concat_axis=0, tiled=True),
        w_gate,
        w_up,
        w_down,
    )
    lookup = (
        returned[flat_expert, position].astype(jnp.float32).reshape(streams_here, chosen, features)
    )
    mixture = jnp.sum(gate_weights[:, :, None] * lookup, axis=1)
    hidden = (thinker_rows.astype(jnp.float32) + mixture).astype(jnp.bfloat16)
    slots = talker_slot[0]
    per_owner = streams_here // devices
    talker_rows = project(hidden, talker_proj)
    placed = (
        jnp.zeros_like(talker_rows)
        .at[slots]
        .set(talker_rows)
        .reshape(devices, per_owner, talker_rows.shape[1])
    )
    return lax.all_to_all(placed, "ep", split_axis=0, concat_axis=0, tiled=True).reshape(
        streams_here, talker_rows.shape[1]
    )


def dense_kernel(
    n,
    rows_hbm,
    ids_hbm,
    gates_hbm,
    slot_hbm,
    count_hbm,
    context_hbm,
    offset_hbm,
    taps_hbm,
    wg_hbm,
    wu_hbm,
    wd_hbm,
    proj_hbm,
    voice_ref,
    rows_ref,
    ids_ref,
    gates_ref,
    slot_ref,
    count_ref,
    context,
    frame_offset,
    taps,
    base_voice,
    voices,
    wg,
    wu,
    wd,
    proj,
    x_all,
    inner,
    grouped,
    part,
    sib_in,
    pair_out,
    y_in,
    y_out,
    z_in,
    load_sem,
    gz_send,
    gz_recv,
    gy_send,
    gy_recv,
    gs_send,
    gs_recv,
    rs_send,
    rs_recv,
    ry_send,
    ry_recv,
    rz_send,
    rz_recv,
):
    f32, bf16 = jnp.float32, jnp.bfloat16
    rows, feat = rows_hbm.shape
    hid = wg.shape[1]
    width = proj.shape[1]
    line = n // 4
    half = line * rows
    tile = min(256, hid)
    me = lax.axis_index("ep")
    z = me // 4
    within = me % 4
    y = within // 2
    core = within % 2
    y_peer = me + 2 - 4 * y
    sibling = me + 1 - 2 * core

    def block(section, pos):
        return pl.ds(pl.multiple_of(section * half + pos * rows, rows), rows)

    own = block(0, z)
    loads = [
        pltpu.make_async_copy(src, dst, load_sem.at[i])
        for i, (src, dst) in enumerate(
            (
                (rows_hbm, rows_ref),
                (ids_hbm, ids_ref),
                (gates_hbm, gates_ref),
                (slot_hbm, slot_ref),
                (count_hbm, count_ref),
                (context_hbm, context),
                (offset_hbm, frame_offset),
                (taps_hbm, taps),
                (wg_hbm.at[0], wg),
                (wu_hbm.at[0], wu),
                (wd_hbm.at[0], wd),
                (proj_hbm, proj),
            )
        )
    ]
    for load in loads[:4]:
        load.start()

    z_peers = [lax.rem(z + k, line) * 4 + within for k in range(1, line)]
    partners = z_peers + [y_peer, sibling]
    barrier = pltpu.get_barrier_semaphore()
    for peer in partners:
        pl.semaphore_signal(barrier, inc=1, device_id={"ep": peer})

    extra = x_all.shape[1] - feat
    spot = lax.broadcasted_iota(jnp.int32, (extra, rows), 0)
    expert_of = lax.rem(spot, n)
    weight = jnp.zeros((extra, rows), f32)
    for load in loads[:4]:
        load.wait()
    for j in range(ids_ref.shape[0]):
        weight = weight + jnp.where(
            ids_ref[j : j + 1, :] == expert_of, gates_ref[j : j + 1, :], 0.0
        )
    high = weight.astype(bf16).astype(f32)
    mid = (weight - high).astype(bf16).astype(f32)
    low = weight - high - mid
    coded = jnp.where(spot < n, high, jnp.where(spot < 2 * n, mid, jnp.where(spot < 3 * n, low, 0.0)))
    owner = lax.broadcasted_iota(jnp.int32, (n, rows), 0)
    pick = jnp.where(owner == slot_ref[...], 1.0, 0.0).astype(bf16)
    x_all[own, :feat] = jnp.dot(pick, rows_ref[...], preferred_element_type=f32).astype(bf16)
    x_all[own, feat:] = lax.dot_general(
        pick, coded.astype(bf16), (((1,), (1,)), ((), ())), preferred_element_type=f32
    ).astype(bf16)

    pl.semaphore_wait(barrier, len(partners))

    def remote(src, dst, send, recv, peer):
        return pltpu.make_async_remote_copy(
            src_ref=src, dst_ref=dst, send_sem=send, recv_sem=recv, device_id={"ep": peer}
        )

    def z_copy(peer, src):
        here = x_all.at[block(0, src)]
        return remote(here, here, gz_send.at[peer], gz_recv.at[src], peer * 4 + within)

    def y_copy(src):
        return remote(
            x_all.at[block(0, src)],
            x_all.at[block(2, src)],
            gy_send.at[src],
            gy_recv.at[src],
            y_peer,
        )

    def s_copy(section, src):
        return remote(
            x_all.at[block(2 * section, src)],
            x_all.at[block(2 * section + 1, src)],
            gs_send.at[section, src],
            gs_recv.at[section, src],
            sibling,
        )

    def at_distance(d, use):
        for src in (z,) if d == 0 else (z - d, z + d):
            pl.when((src >= 0) & (src < line))(functools.partial(use, src))

    def to_z(d, act):
        at_distance(d, lambda peer: act(z_copy(peer, z)))

    def from_z(d):
        at_distance(d, lambda src: z_copy(src, src).wait_recv())

    def hand_on(src):
        y_copy(src).start()
        s_copy(0, src).start()

    def from_y(src):
        y_copy(src).wait_recv()
        s_copy(1, src).start()

    to_z(1, lambda copy: copy.start())
    hand_on(z)
    for d in range(2, line):
        to_z(d, lambda copy: copy.start())
    for load in loads[4:]:
        load.start()

    for load in loads[4:8]:
        load.wait()
    before = context.shape[0]
    horizon = frame_offset.shape[0]
    for f in range(horizon):
        voice = jnp.zeros((rows, width), f32)
        for t in range(taps.shape[0]):
            tap = taps[t : t + 1, :]
            if f + t < before:
                voice = voice + tap * context[f + t].astype(f32)
            else:
                voice = voice + tap * frame_offset[f + t - before : f + t - before + 1, :]
        base_voice[f] = voice

    for d in range(1, line):
        from_z(d)
        at_distance(d, hand_on)
        if d < line - 1:
            at_distance(d - 1, from_y)

    loads[8].wait()
    loads[9].wait()

    def up_pass(base):
        span = pl.ds(base, 2 * half)
        lanes = lax.broadcasted_iota(jnp.int32, (2 * half, extra), 1)
        mine = (lax.rem(lanes, n) == me) & (lanes < 3 * n)
        coef = jnp.sum(
            jnp.where(mine, x_all[span, feat:].astype(f32), 0.0), axis=1, keepdims=True
        )

        def step(j, carry):
            cols = pl.ds(pl.multiple_of(j * tile, tile), tile)
            x = x_all[span, :feat]
            gate_act = jnp.dot(x, wg[:, cols], preferred_element_type=f32)
            up_act = jnp.dot(x, wu[:, cols], preferred_element_type=f32)
            inner[span, cols] = (jax.nn.silu(gate_act) * up_act * coef).astype(bf16)
            return carry

        lax.fori_loop(0, hid // tile, step, 0)

    def place(index):
        section = index // half
        device = (
            (index % half) // rows * 4
            + jnp.where(section // 2 == 0, y, 1 - y) * 2
            + jnp.where(section % 2 == 0, core, 1 - core)
        )
        return device, index % rows

    def regroup():
        every = n * rows
        row_owner, row_source = place(lax.broadcasted_iota(jnp.int32, (every, 1), 0))
        col_source, col_owner = place(lax.broadcasted_iota(jnp.int32, (1, every), 1))
        match = (row_owner == col_owner) & (row_source == col_source)
        return jnp.where(match, 1.0, 0.0).astype(bf16)

    def down_pass(base, cut):
        span = pl.ds(base, 2 * half)

        def step(j, carry):
            cols = pl.ds(pl.multiple_of(cut * piece + j * tile, tile), tile)
            out = jnp.dot(grouped[span, :], wd[:, cols], preferred_element_type=f32)
            part[span, cols] = out.astype(bf16)
            return carry

        lax.fori_loop(0, piece // tile, step, 0)

    cuts = rs_send.shape[1]
    piece = feat // cuts

    def columns(cut):
        return pl.ds(cut * piece, piece)

    reduce_s = [
        [
            remote(
                part.at[pl.ds((2 * section + 1) * half, half), columns(cut)],
                sib_in.at[pl.ds(section * half, half), columns(cut)],
                rs_send.at[section, cut],
                rs_recv.at[section, cut],
                sibling,
            )
            for cut in range(cuts)
        ]
        for section in range(2)
    ]
    for src in range(line):
        s_copy(0, src).wait_recv()
    up_pass(0)
    for d in range(max(line - 2, 0), line):
        at_distance(d, from_y)
    order = regroup()
    for src in range(line):
        s_copy(1, src).wait_recv()
    up_pass(2 * half)
    grouped[...] = jnp.dot(order, inner[...], preferred_element_type=f32).astype(bf16)
    loads[10].wait()
    for cut in range(cuts):
        down_pass(2 * half, cut)
        reduce_s[1][cut].start()

    col_source, col_owner = place(lax.broadcasted_iota(jnp.int32, (1, n * rows), 1))
    source = lax.broadcasted_iota(jnp.int32, (rows, 1), 0)
    keep = jnp.where((col_source == source) & (col_owner == me), 1.0, 0.0).astype(bf16)

    def target(k):
        return lax.rem(z + k, line)

    reduce_y = [
        [
            remote(
                pair_out.at[block(0, target(k)), columns(cut)],
                y_in.at[block(0, target(k)), columns(cut)],
                ry_send.at[k, cut],
                ry_recv.at[k, cut],
                y_peer,
            )
            for cut in range(cuts)
        ]
        for k in range(line)
    ]
    reduce_z = [
        [
            remote(
                y_out.at[block(0, target(k)), columns(cut)],
                z_in.at[block(0, k), columns(cut)],
                rz_send.at[k, cut],
                rz_recv.at[k, cut],
                target(k) * 4 + within,
            )
            for cut in range(cuts)
        ]
        for k in range(1, line)
    ]

    def to_y(k, cut):
        cols = columns(cut)
        mine, theirs = block(2, target(k)), block(1, target(k))
        pair_out[block(0, target(k)), cols] = (
            part[mine, cols].astype(f32) + sib_in[theirs, cols].astype(f32)
        ).astype(bf16)
        reduce_y[k][cut].start()

    for cut in range(cuts):
        down_pass(0, cut)
        reduce_s[0][cut].start()
        reduce_s[1][cut].wait_recv()
        for k in range(1, line):
            to_y(k, cut)
    for cut in range(cuts):
        to_y(0, cut)
    for cut in range(cuts):
        cols = columns(cut)
        reduce_s[0][cut].wait_recv()
        for k in range(1, line):
            here = block(0, target(k))
            reduce_y[k][cut].wait_recv()
            y_out[here, cols] = (
                part[here, cols].astype(f32)
                + sib_in[here, cols].astype(f32)
                + y_in[here, cols].astype(f32)
            ).astype(bf16)
            reduce_z[k - 1][cut].start()
    residual = jnp.dot(keep, x_all[:, :feat], preferred_element_type=f32)
    for cut in range(cuts):
        reduce_y[0][cut].wait_recv()
    total = (
        residual
        + part[own, :].astype(f32)
        + sib_in[own, :].astype(f32)
        + y_in[own, :].astype(f32)
    )
    for k in range(1, line):
        for cut in range(cuts):
            reduce_z[k - 1][cut].wait_recv()
        total = total + z_in[k * rows : (k + 1) * rows, :].astype(f32)
    hidden = total.astype(bf16).astype(f32)
    scale = lax.rsqrt(jnp.mean(hidden * hidden, axis=-1, keepdims=True) + 1e-06)
    normed = (hidden * scale).astype(bf16)

    loads[11].wait()
    diagonal = lax.broadcasted_iota(jnp.int32, (rows, rows), 0) == lax.broadcasted_iota(
        jnp.int32, (rows, rows), 1
    )
    count = jnp.sum(
        jnp.where(diagonal, count_ref[...].astype(f32), 0.0), axis=1, keepdims=True
    )
    for j in range(width // tile):
        cols = slice(j * tile, (j + 1) * tile)
        talk = jnp.dot(normed, proj[:, cols], preferred_element_type=f32)
        owned = talk.astype(bf16).astype(f32)
        for f in range(horizon):
            gain = jnp.sum(taps[before - f :, cols], axis=0, keepdims=True)
            voice = base_voice[f, :, cols] + gain * owned
            voices[:, f, cols] = jnp.where(count > f, voice, 0.0)
        voice_ref[:, :, cols] = voices[:, :, cols].astype(bf16)

    for d in range(1, line):
        to_z(d, lambda copy: copy.wait_send())
    for src in range(line):
        y_copy(src).wait_send()
        s_copy(0, src).wait_send()
        s_copy(1, src).wait_send()
    for group in reduce_s + reduce_y + reduce_z:
        for copy in group:
            copy.wait_send()


def dense_path(
    thinker_rows,
    expert_ids,
    gate_weights,
    w_gate,
    w_up,
    w_down,
    talker_proj,
    talker_slot,
    speech_count,
    left_context,
    frame_offset,
    conv_weight,
):
    n = lax.axis_size("ep")
    rows, feat = thinker_rows.shape
    hid = w_gate.shape[2]
    width = talker_proj.shape[1]
    line = n // 4
    every = n * rows
    extra = -(-3 * n // LANES) * LANES
    bf16, f32 = jnp.bfloat16, jnp.float32
    chosen = expert_ids.shape[1]
    before = left_context.shape[1]
    horizon = frame_offset.shape[0]
    cuts = 4
    vmem = pl.BlockSpec(memory_space=pltpu.VMEM)
    hbm = pl.BlockSpec(memory_space=pl.ANY)
    dma = pltpu.SemaphoreType.DMA
    return pl.pallas_call(
        functools.partial(dense_kernel, n),
        out_shape=jax.ShapeDtypeStruct((rows, horizon, width), bf16),
        in_specs=[hbm] * 12,
        out_specs=vmem,
        scratch_shapes=[
            pltpu.VMEM((rows, feat), bf16),
            pltpu.VMEM((chosen, rows), jnp.int32),
            pltpu.VMEM((chosen, rows), f32),
            pltpu.VMEM((1, rows), jnp.int32),
            pltpu.VMEM((1, rows), jnp.int32),
            pltpu.VMEM((before, rows, width), bf16),
            pltpu.VMEM((horizon, width), f32),
            pltpu.VMEM(conv_weight.shape, f32),
            pltpu.VMEM((horizon, rows, width), f32),
            pltpu.VMEM((rows, horizon, width), f32),
            pltpu.VMEM((feat, hid), bf16),
            pltpu.VMEM((feat, hid), bf16),
            pltpu.VMEM((hid, feat), bf16),
            pltpu.VMEM((feat, width), bf16),
            pltpu.VMEM((every, feat + extra), bf16),
            pltpu.VMEM((every, hid), bf16),
            pltpu.VMEM((every, hid), bf16),
            pltpu.VMEM((every, feat), bf16),
            pltpu.VMEM((every // 2, feat), bf16),
            pltpu.VMEM((line * rows, feat), bf16),
            pltpu.VMEM((line * rows, feat), bf16),
            pltpu.VMEM((line * rows, feat), bf16),
            pltpu.VMEM((line * rows, feat), bf16),
            dma((12,)),
            dma((line,)),
            dma((line,)),
            dma((line,)),
            dma((line,)),
            dma((2, line)),
            dma((2, line)),
            dma((2, cuts)),
            dma((2, cuts)),
            dma((line, cuts)),
            dma((line, cuts)),
            dma((line, cuts)),
            dma((line, cuts)),
        ],
        compiler_params=pltpu.CompilerParams(
            collective_id=0, has_side_effects=True, vmem_limit_bytes=60 * 1024 * 1024
        ),
    )(
        thinker_rows,
        expert_ids.T,
        gate_weights.T,
        talker_slot,
        speech_count.reshape(1, rows),
        left_context.transpose(1, 0, 2),
        frame_offset,
        conv_weight,
        w_gate,
        w_up,
        w_down,
        talker_proj,
    )


def local(
    thinker_rows,
    expert_ids,
    gate_weights,
    w_gate,
    w_up,
    w_down,
    talker_proj,
    talker_slot,
    speech_count,
    left_context,
    frame_offset,
    conv_weight,
):
    devices = lax.axis_size("ep")
    streams_here = thinker_rows.shape[0]
    dense = streams_here <= CAP and streams_here == devices and devices % 4 == 0
    experts = (
        thinker_rows, expert_ids, gate_weights, w_gate, w_up, w_down, talker_proj, talker_slot
    )
    voices = (speech_count, left_context, frame_offset, conv_weight)
    if dense:
        return dense_path(*experts, *voices)
    return vocode(capacity_path(*experts), *voices)


def solution(mesh):
    in_specs = (
        P(("groups", "ep"), None),
        P(("groups", "ep"), None),
        P(("groups", "ep"), None),
        P("ep", None, None),
        P("ep", None, None),
        P("ep", None, None),
        P(),
        P(("groups", "ep"), None),
        P(("groups", "ep")),
        P(("groups", "ep"), None, None),
        P(),
        P(),
    )
    out_specs = P(("groups", "ep"), None, None)
    return jax.shard_map(local, mesh=mesh, in_specs=in_specs, out_specs=out_specs, check_vma=False)
```
